32 devices in a mesh: section: 4 (over y, core), seq: 8 (over z, x).
Axes of the slice: x: 2, y: 2, z: 4, core: 2. Of those that a mesh axis runs over, the one named last changes fastest.
Arguments:
- base_ids: int32 [2, 1024], P(None, 'seq'), may hold values from 0 to 3
- stem_weight: bfloat16 [15, 4, 768], replicated, may hold values from -1.5 to 1.5
- conv_weight: bfloat16 [4, 5, 768, 768], P('section'), may hold values from -0.09375 to 0.09375
- block_gain: float32 [4, 768], P('section'), may hold values from 0.1 to 1.9
- cotangent: bfloat16 [2, 1024, 768], P(None, 'seq'), may hold values from -0.29882812 to 0.29882812
Outputs:
- conv_grad: bfloat16 [4, 5, 768, 768], P('section', None, 'seq')
- gain_grad: float32 [4, 768], P('section', 'seq')
The draws below stay inside these ranges and needn't reach their ends.
All inputs are finite; a program needn't handle non-finite values.
Results may differ from the reference program's by a relative error of at most 0.035.
Values may be sent and summed in bfloat16 or wider, within the bound.
A program may use at most 128 MiB of HBM per device.

```python
import jax
import jax.numpy as jnp
from jax import lax

C = 768
KERNEL = 5
STEM_K = 15
BASES = 4
MICRO = 2
TOK_DEV = 128
TOKENS = 1024
N_SECTION = 4
N_SEQ = 8


def plant(values, stream_key, least, largest):
    longest = values.shape.index(max(values.shape))
    spots = []
    for shift in (0, 1):
        where = [jax.random.randint(jax.random.fold_in(stream_key, axis), (), 0, length) for axis, length in enumerate(values.shape)]
        where[longest] = (where[longest] + shift) % values.shape[longest]
        spots.append(tuple(where))
    return values.at[spots[0]].set(least).at[spots[1]].set(largest)


def block_scale(rng, dims, cuts, low, largest):
    factor_of, own = 1.0, jax.random.fold_in(rng, 6)
    for position, blocks in cuts:
        heights = jnp.exp(jax.random.uniform(jax.random.fold_in(own, position), (blocks,), jnp.float32, low / len(cuts), largest / len(cuts)))
        factor_of = factor_of * jnp.repeat(heights, dims[position] // blocks).reshape([-1 if axis == position else 1 for axis in range(len(dims))])
    return factor_of


def bell_draw(key, shape, deviation, reach, split=(), kind=jnp.bfloat16):
    level = block_scale(key, shape, split, -0.22, 0.18) if split else 1.0
    result = jax.random.normal(key, shape, jnp.float32) * deviation * level
    return jnp.minimum(jnp.maximum(result, -reach), reach).astype(kind)


def setup_inputs(seed: int = 0) -> dict:
    key_of = jax.random.split(jax.random.key(seed), 6)
    return {
        "base_ids": plant(jax.random.randint(key_of[0], (MICRO, TOKENS), 0, 4), jax.random.fold_in(key_of[0], 1), 0, 3).astype(jnp.int32),
        "stem_weight": bell_draw(key_of[1], (STEM_K, BASES, C), STEM_K ** -0.5, 1.5),
        "conv_weight": bell_draw(key_of[2], (N_SECTION, KERNEL, C, C), (KERNEL * C) ** -0.5, 0.09375, ((0, 4),)),
        "block_gain": jnp.clip(1.0 + 0.18 * jax.random.normal(key_of[3], (N_SECTION, C), jnp.float32), 0.1, 1.9),
        "cotangent": bell_draw(key_of[4], (MICRO, TOKENS, C), 0.05, 0.29882812, ((1, 8),)),
    }


def activate(block_sum, gain_row):
    scale = lax.rsqrt(lax.optimization_barrier(jnp.mean(block_sum * block_sum, axis=-1, keepdims=True)) + 1e-06)
    return jax.nn.gelu(block_sum * scale * gain_row)

def rounded_sum(partials):
    held = lax.optimization_barrier(partials.astype(jnp.bfloat16))
    return lax.optimization_barrier(jnp.sum(held.astype(jnp.float32), axis=0))

def conv_apply(activated, filters):
    row_count = activated.shape[1]
    conv_reach = (KERNEL - 1) // 2
    padded = jnp.pad(activated, ((0, 0), (conv_reach, conv_reach), (0, 0))).astype(jnp.float32)
    summed = jnp.zeros(activated.shape, jnp.float32)
    for offset in range(KERNEL):
        summed = summed + jnp.einsum('mtc,cd->mtd', padded[:, offset:offset + row_count], filters[offset].astype(jnp.float32))
    return summed

def conv_back(grad_out, filters):
    row_count = grad_out.shape[1]
    conv_reach = (KERNEL - 1) // 2
    padded = jnp.pad(grad_out, ((0, 0), (conv_reach, conv_reach), (0, 0))).astype(jnp.float32)
    summed = jnp.zeros(grad_out.shape, jnp.float32)
    for offset in range(KERNEL):
        start = 2 * conv_reach - offset
        summed = summed + jnp.einsum('mtd,cd->mtc', padded[:, start:start + row_count], filters[offset].astype(jnp.float32))
    return summed

def reference(base_ids, stem_weight, conv_weight, block_gain, cotangent):
    micro_count = base_ids.shape[0]
    total_rows = base_ids.shape[1]
    section_count = conv_weight.shape[0]
    half_count = section_count // 2
    conv_reach = (KERNEL - 1) // 2
    stem_reach = (STEM_K - 1) // 2
    padded_ids = jnp.pad(base_ids + 1, ((0, 0), (stem_reach, stem_reach)))
    letters = jnp.arange(1, BASES + 1, dtype=jnp.int32)
    stem_sum = jnp.zeros((micro_count, total_rows, C), jnp.float32)
    for offset in range(STEM_K):
        onehot = (padded_ids[:, offset:offset + total_rows, None] == letters).astype(jnp.float32)
        stem_sum = stem_sum + jnp.einsum('mtb,bc->mtc', onehot, stem_weight[offset].astype(jnp.float32))
    stream = stem_sum.astype(jnp.bfloat16)
    skip_list = []
    saved = []
    for block_index in range(section_count):
        block_sum = stream.astype(jnp.float32)
        if block_index >= half_count:
            block_sum = block_sum + skip_list[section_count - 1 - block_index].astype(jnp.float32)
        activated = activate(block_sum, block_gain[block_index]).astype(jnp.bfloat16)
        stream = (block_sum + conv_apply(activated, conv_weight[block_index])).astype(jnp.bfloat16)
        saved.append((block_sum, activated))
        if block_index < half_count:
            skip_list.append(stream)
    grad_flow = cotangent
    skip_grads = [None] * half_count
    kernel_grads = [None] * section_count
    gain_grads = [None] * section_count
    shape_four = (micro_count, N_SEQ, TOK_DEV, C)
    for block_index in reversed(range(section_count)):
        block_sum, activated = saved[block_index]
        from_next = grad_flow.astype(jnp.float32)
        if block_index < half_count:
            from_next = from_next + skip_grads[block_index].astype(jnp.float32)
        grad_out = from_next.astype(jnp.bfloat16)
        grad_act = conv_back(grad_out, conv_weight[block_index])
        padded = jnp.pad(activated, ((0, 0), (conv_reach, conv_reach), (0, 0))).astype(jnp.float32)
        grad_four = grad_out.astype(jnp.float32).reshape(shape_four)
        per_offset = []
        for offset in range(KERNEL):
            window = padded[:, offset:offset + total_rows].reshape(shape_four)
            per_offset.append(rounded_sum(jnp.einsum('mqtc,mqtd->qcd', window, grad_four)))
        kernel_grads[block_index] = jnp.stack(per_offset)

        def blockwise(sum_four, gain_rows):
            return activate(sum_four, gain_rows[None, :, None, :])
        gain_rows = jnp.broadcast_to(block_gain[block_index], (N_SEQ, C))
        unused_out, pullback = jax.vjp(blockwise, block_sum.reshape(shape_four), gain_rows)
        grad_norm_in, grad_gain = pullback(grad_act.reshape(shape_four))
        gain_grads[block_index] = rounded_sum(grad_gain)
        grad_in = (grad_out.astype(jnp.float32) + grad_norm_in.reshape(block_sum.shape)).astype(jnp.bfloat16)
        if block_index >= half_count:
            skip_grads[section_count - 1 - block_index] = grad_in
        grad_flow = grad_in
    conv_grad = jnp.stack(kernel_grads).astype(jnp.bfloat16)
    gain_grad = jnp.stack(gain_grads)
    return (conv_grad, gain_grad)
```

```python
import functools

import jax
import jax.numpy as jnp
from jax import lax
from jax.experimental import pallas as pl
from jax.experimental.pallas import tpu as pltpu
from jax.sharding import PartitionSpec as P

KERNEL = 5
STEM_K = 15
BASES = 4
LANES = 128
EDGE = 8
F32, BF16 = jnp.float32, jnp.bfloat16
GELU_A, GELU_B = 0.7978845608028654, 0.044715


def remote(src, dst, send_sem, recv_sem, **where):
    return pltpu.make_async_remote_copy(
        src_ref=src,
        dst_ref=dst,
        send_sem=send_sem,
        recv_sem=recv_sem,
        device_id=where,
        device_id_type=pl.DeviceIdType.MESH,
    )


def level_kernel(
    sections, n_seq, n_lo, micro, rows, chans, halo,
    e_ref, stem_ref, w_ref, gain_ref, cot_ref,
    out_ref, gout_ref,
    ebuf, bsum, actf, x5, gradf, gact, inflow, skip, fout, gin, gskip, gsend, coth,
    aslab, acol, acolf, a5t, gall, acc, gain_acc, gslab, grecv,
    e_send, e_recv, c_send, c_recv, f_send, f_recv, b_send, b_recv,
    a_send, a_recv, n_send, n_recv, ag_send, ag_recv,
):
    sec, q = lax.axis_index("section"), lax.axis_index("seq")
    n_hi = n_seq // n_lo
    hi, lo = q // n_lo, q % n_lo
    half = sections // 2
    ext = rows + 2 * halo
    e_halo = halo + 16
    part = chans // n_seq
    reach = (KERNEL - 1) // 2
    last = sections - 1
    mirror_sec = last - sec
    step = 32
    tokens = rows * n_seq

    barrier = pltpu.get_barrier_semaphore()
    for d in range(1, n_seq):
        pl.semaphore_signal(
            barrier, inc=1, device_id={"seq": (q + d) % n_seq}, device_id_type=pl.DeviceIdType.MESH
        )
    for d in range(1, sections):
        pl.semaphore_signal(
            barrier, inc=1, device_id={"section": (sec + d) % sections},
            device_id_type=pl.DeviceIdType.MESH,
        )
    pl.semaphore_wait(barrier, n_seq + sections - 2)

    def e_copy(side):
        if side == 0:
            src, dst, to = e_ref.at[:, rows - e_halo : rows], ebuf.at[:, 0:e_halo], q + 1
        else:
            src, dst, to = e_ref.at[:, 0:e_halo], ebuf.at[:, e_halo + rows :], q - 1
        return remote(src, dst, e_send.at[side], e_recv.at[side], seq=to)

    def c_copy(side):
        if side == 0:
            src, dst, to = cot_ref.at[:, rows - halo : rows], coth.at[0], q + 1
        else:
            src, dst, to = cot_ref.at[:, 0:halo], coth.at[1], q - 1
        return remote(src, dst, c_send.at[side], c_recv.at[side], seq=to)

    def gather_copy(block, m, way):
        to = [q + n_lo, q - n_lo, q + 1, q - 1][way]
        return remote(
            gall.at[block, m], gall.at[block, m], ag_send.at[block, m, way],
            ag_recv.at[block, m], seq=to,
        )

    up, down, right, left = hi < n_hi - 1, hi > 0, lo < n_lo - 1, lo > 0

    def each_way(ways, block, m, act):
        for way in ways:
            @pl.when([up, down, right, left][way])
            def _():
                act(gather_copy(block, m, way))

    def start(copy):
        copy.start()

    def wait_send(copy):
        copy.wait_send()

    for ref in (actf, gradf):
        ref[:, 0:EDGE] = jnp.zeros((micro, EDGE, chans), F32)
        ref[:, EDGE + ext :] = jnp.zeros((micro, EDGE, chans), F32)
    acolf[:, 0:EDGE] = jnp.zeros((micro, EDGE, LANES), F32)
    acolf[:, EDGE + tokens :] = jnp.zeros((micro, EDGE, LANES), F32)
    gain_acc[...] = jnp.zeros_like(gain_acc)

    @pl.when(sec == 0)
    def _():
        @pl.when(q < n_seq - 1)
        def _():
            e_copy(0).start()

        @pl.when(q > 0)
        def _():
            e_copy(1).start()

        ebuf[:, e_halo : e_halo + rows] = e_ref[...]

        @pl.when(q == 0)
        def _():
            ebuf[:, 0:e_halo] = jnp.zeros((micro, e_halo, LANES), F32)

        @pl.when(q == n_seq - 1)
        def _():
            ebuf[:, e_halo + rows :] = jnp.zeros((micro, e_halo, LANES), F32)

        @pl.when(q > 0)
        def _():
            e_copy(0).wait_recv()

        @pl.when(q < n_seq - 1)
        def _():
            e_copy(1).wait_recv()

    def row_mask(first, count):
        place = lax.broadcasted_iota(jnp.int32, (count, 1), 0) + (first + q * rows - halo)
        return (place >= 0) & (place < tokens)

    def shifted(ref, m, flip):
        for k in range(KERNEL):
            off = EDGE + (reach - k if flip else k - reach)
            x5[:, k * chans : (k + 1) * chans] = ref[m, off : off + ext].astype(BF16)

    def conv_back(m):
        shifted(gradf, m, True)

        def tile(n, carry):
            at = pl.ds(pl.multiple_of(n * 256, 256), 256)
            total = jnp.zeros((ext, 256), F32)
            for k in range(KERNEL):
                total = total + lax.dot_general(
                    x5[:, k * chans : (k + 1) * chans],
                    w_ref[pl.ds(pl.multiple_of(k * chans + n * 256, 256), 256), :],
                    (((1,), (1,)), ((), ())),
                    preferred_element_type=F32,
                )
            gact[m, :, at] = total
            return carry

        lax.fori_loop(0, chans // 256, tile, 0)

    @pl.when(sec == last)
    def _():
        @pl.when(q < n_seq - 1)
        def _():
            c_copy(0).start()

        @pl.when(q > 0)
        def _():
            c_copy(1).start()

        gall[q] = cot_ref[...]
        for m in range(micro):
            each_way(range(4), q, m, start)
        gradf[:, EDGE + halo : EDGE + halo + rows] = cot_ref[...].astype(F32)

        @pl.when(q == 0)
        def _():
            gradf[:, EDGE : EDGE + halo] = jnp.zeros((micro, halo, chans), F32)

        @pl.when(q == n_seq - 1)
        def _():
            gradf[:, EDGE + halo + rows : EDGE + ext] = jnp.zeros((micro, halo, chans), F32)

        @pl.when(q > 0)
        def _():
            c_copy(0).wait_recv()
            gradf[:, EDGE : EDGE + halo] = coth[0].astype(F32)

        @pl.when(q < n_seq - 1)
        def _():
            c_copy(1).wait_recv()
            gradf[:, EDGE + halo + rows : EDGE + ext] = coth[1].astype(F32)

        def each(m, carry):
            conv_back(m)
            return carry

        lax.fori_loop(0, micro, each, 0)

    def f_copy(m, kind):
        to = sec + 1 if kind == 0 else mirror_sec
        dst = inflow if kind == 0 else skip
        return remote(fout.at[m], dst.at[m], f_send.at[m, kind], f_recv.at[m, kind], section=to)

    def b_copy(m, kind):
        to = sec - 1 if kind == 0 else mirror_sec
        dst = gin if kind == 0 else gskip
        return remote(gsend.at[m], dst.at[m], b_send.at[m, kind], b_recv.at[m, kind], section=to)

    def by_rows(body):
        def one(i, carry):
            body(pl.multiple_of(i * step, step))
            return carry

        lax.fori_loop(0, ext // step, one, 0)

    def forward(m, carry):
        @pl.when(sec == 0)
        def _():
            tap = lax.broadcasted_iota(jnp.int32, (ext, LANES), 1) // BASES
            hot = jnp.zeros((ext, LANES), F32)
            for k in range(STEM_K):
                off = e_halo - halo + k - (STEM_K - 1) // 2
                hot = jnp.where(tap == k, ebuf[m, off : off + ext], hot)
            stem = jnp.dot(hot.astype(BF16), stem_ref[...], preferred_element_type=F32)
            bsum[m] = stem.astype(BF16).astype(F32)

        @pl.when(sec > 0)
        def _():
            f_copy(m, 0).wait_recv()

            @pl.when(sec < half)
            def _():
                bsum[m] = inflow[m].astype(F32)

            @pl.when(sec == half)
            def _():
                bsum[m] = inflow[m].astype(F32) * 2.0

            @pl.when(sec > half)
            def _():
                f_copy(m, 1).wait_recv()
                bsum[m] = inflow[m].astype(F32) + skip[m].astype(F32)

        def act_rows(r):
            b = bsum[m, pl.ds(r, step)]
            scale = lax.rsqrt(jnp.mean(b * b, axis=-1, keepdims=True) + 1e-06)
            x = b * scale * gain_ref[...]
            t = jnp.tanh(GELU_A * (x + GELU_B * (x * x * x)))
            y = (x * (0.5 * (1.0 + t))).astype(BF16).astype(F32)
            actf[m, pl.ds(pl.multiple_of(EDGE + r, 8), step)] = jnp.where(row_mask(r, step), y, 0.0)

        by_rows(act_rows)

        @pl.when(sec < last)
        def _():
            shifted(actf, m, False)

            def tile(n, c):
                at = pl.ds(pl.multiple_of(n * 256, 256), 256)
                total = bsum[m, :, at] + jnp.dot(
                    x5[...], w_ref[:, at], preferred_element_type=F32
                )
                fout[m, :, at] = total.astype(BF16)
                return c

            lax.fori_loop(0, chans // 256, tile, 0)
            f_copy(m, 0).start()

            @pl.when(sec < half - 1)
            def _():
                f_copy(m, 1).start()

        return carry

    lax.fori_loop(0, micro, forward, 0)

    def picker(j):
        c = lax.broadcasted_iota(jnp.int32, (chans, LANES), 0)
        lane = lax.broadcasted_iota(jnp.int32, (chans, LANES), 1)
        return jnp.where((c == j * part + lane) & (lane < part), 1.0, 0.0).astype(BF16)

    def a_copy(j):
        return remote(aslab.at[j], acol.at[q], a_send.at[j], a_recv.at[q], seq=j)

    def a_from(j):
        return remote(aslab.at[j], acol.at[j], a_send.at[j], a_recv.at[j], seq=j)

    def spread_rows():
        own = slice(EDGE + halo, EDGE + halo + rows)

        def slab(j, carry):
            pick = picker(j)
            for m in range(micro):
                aslab[j, m] = jnp.dot(
                    actf[m, own].astype(BF16), pick, preferred_element_type=F32
                ).astype(BF16)

            @pl.when(j != q)
            def _():
                a_copy(j).start()

            @pl.when(j == q)
            def _():
                acol[j] = aslab[j]

            return carry

        lax.fori_loop(0, n_seq, slab, 0)

        def take(j, carry):
            @pl.when(j != q)
            def _():
                a_from(j).wait_recv()

            at = pl.ds(pl.multiple_of(EDGE + j * rows, 8), rows)
            for m in range(micro):
                acolf[m, at] = acol[j, m].astype(F32)
            return carry

        lax.fori_loop(0, n_seq, take, 0)

        def turn(j, carry):
            for m in range(micro):
                window = acolf[m, pl.ds(pl.multiple_of(j * rows, rows), rows + 2 * EDGE)]
                for k in range(KERNEL):
                    off = EDGE + k - reach
                    a5t[j, k * LANES : (k + 1) * LANES, m * rows : (m + 1) * rows] = (
                        window[off : off + rows].T.astype(BF16)
                    )
            return carry

        lax.fori_loop(0, n_seq, turn, 0)

    @pl.when(sec < half)
    def _():
        spread_rows()

    def backward(m, carry):
        @pl.when(sec < last)
        def _():
            b_copy(m, 0).wait_recv()

            @pl.when(sec < half - 1)
            def _():
                b_copy(m, 1).wait_recv()
                gradf[m, EDGE : EDGE + ext] = (
                    (gin[m].astype(F32) + gskip[m].astype(F32)).astype(BF16).astype(F32)
                )

            @pl.when(sec == half - 1)
            def _():
                gradf[m, EDGE : EDGE + ext] = gin[m].astype(F32) * 2.0

            @pl.when(sec >= half)
            def _():
                gradf[m, EDGE : EDGE + ext] = gin[m].astype(F32)

            gall[q, m] = gradf[m, EDGE + halo : EDGE + halo + rows].astype(BF16)
            each_way(range(4), q, m, start)
            conv_back(m)

        def pull_rows(r):
            at = pl.ds(r, step)
            b, grad = bsum[m, at], gact[m, at]
            scale = lax.rsqrt(jnp.mean(b * b, axis=-1, keepdims=True) + 1e-06)
            unit = b * scale
            x = unit * gain_ref[...]
            t = jnp.tanh(GELU_A * (x + GELU_B * (x * x * x)))
            slope = 0.5 * (1.0 + t) + (0.5 * GELU_A) * x * (1.0 - t * t) * (
                1.0 + (3.0 * GELU_B) * (x * x)
            )
            d_pre = grad * slope
            d_unit = d_pre * gain_ref[...]
            place = lax.broadcasted_iota(jnp.int32, (step, 1), 0) + r
            mine = (place >= halo) & (place < halo + rows)
            terms = jnp.where(mine, d_pre * unit, 0.0)
            gain_acc[...] += jnp.sum(terms.reshape(step // 8, 8, chans), axis=0)
            pulled = scale * (d_unit - unit * jnp.mean(d_unit * unit, axis=-1, keepdims=True))
            whole = gradf[m, pl.ds(pl.multiple_of(EDGE + r, 8), step)] + pulled
            gsend[m, at] = jnp.where(row_mask(r, step), whole, 0.0).astype(BF16)

        by_rows(pull_rows)

        @pl.when(sec > 0)
        def _():
            b_copy(m, 0).start()

            @pl.when(sec > half)
            def _():
                b_copy(m, 1).start()

        return carry

    lax.fori_loop(0, micro, backward, 0)

    for d in range(1, n_hi):
        for m in range(micro):
            @pl.when(hi - d >= 0)
            def _():
                block = q - d * n_lo
                gather_copy(block, m, 0).wait_recv()
                each_way((0, 2, 3), block, m, start)

            @pl.when(hi + d < n_hi)
            def _():
                block = q + d * n_lo
                gather_copy(block, m, 1).wait_recv()
                each_way((1, 2, 3), block, m, start)

    @pl.when(sec >= half)
    def _():
        spread_rows()

    def n_copy(j):
        return remote(gslab.at[j], grecv.at[q], n_send.at[j], n_recv.at[q], seq=j)

    def n_from(j):
        return remote(gslab.at[j], grecv.at[j], n_send.at[j], n_recv.at[j], seq=j)

    gain_part = jnp.broadcast_to(jnp.sum(gain_acc[...], axis=0, keepdims=True), (16, chans))
    gain_part = gain_part.astype(BF16)

    def gain_slab(j, carry):
        gslab[j] = jnp.dot(gain_part, picker(j), preferred_element_type=F32)[0:8]

        @pl.when(j != q)
        def _():
            n_copy(j).start()

        @pl.when(j == q)
        def _():
            grecv[j] = gslab[j]

        return carry

    lax.fori_loop(0, n_seq, gain_slab, 0)

    for e in range(1, n_lo):
        for h in range(n_hi):
            for m in range(micro):
                @pl.when(lo - e >= 0)
                def _():
                    block = h * n_lo + lo - e
                    gather_copy(block, m, 2).wait_recv()
                    each_way((2,), block, m, start)

                @pl.when(lo + e < n_lo)
                def _():
                    block = h * n_lo + lo + e
                    gather_copy(block, m, 3).wait_recv()
                    each_way((3,), block, m, start)

    acc[...] = jnp.zeros_like(acc)

    def multiply(j, carry):
        def tile(n, c):
            at = pl.ds(pl.multiple_of(n * 256, 256), 256)
            acc[:, at] += jnp.dot(
                a5t[j], gall[j, :, :, at].reshape(micro * rows, 256), preferred_element_type=F32
            )
            return c

        return lax.fori_loop(0, chans // 256, tile, carry)

    lax.fori_loop(0, n_seq, multiply, 0)
    for k in range(KERNEL):
        out_ref[k] = acc[k * LANES : k * LANES + part].astype(BF16)

    def gain_take(j, total):
        @pl.when(j != q)
        def _():
            n_from(j).wait_recv()

        return total + grecv[j]

    gain_total = lax.fori_loop(0, n_seq, gain_take, jnp.zeros((8, LANES), F32))
    gout_ref[...] = gain_total[0:1, 0:part]

    @pl.when(sec == 0)
    def _():
        @pl.when(q < n_seq - 1)
        def _():
            e_copy(0).wait_send()

        @pl.when(q > 0)
        def _():
            e_copy(1).wait_send()

    @pl.when(sec == last)
    def _():
        @pl.when(q < n_seq - 1)
        def _():
            c_copy(0).wait_send()

        @pl.when(q > 0)
        def _():
            c_copy(1).wait_send()

    for m in range(micro):
        @pl.when(sec < last)
        def _():
            f_copy(m, 0).wait_send()

        @pl.when(sec < half - 1)
        def _():
            f_copy(m, 1).wait_send()

        @pl.when(sec > 0)
        def _():
            b_copy(m, 0).wait_send()

        @pl.when(sec > half)
        def _():
            b_copy(m, 1).wait_send()

        each_way(range(4), q, m, wait_send)
        for d in range(1, n_hi):
            @pl.when(hi - d >= 0)
            def _():
                each_way((0, 2, 3), q - d * n_lo, m, wait_send)

            @pl.when(hi + d < n_hi)
            def _():
                each_way((1, 2, 3), q + d * n_lo, m, wait_send)

        for e in range(1, n_lo):
            for h in range(n_hi):
                @pl.when(lo - e >= 0)
                def _():
                    each_way((2,), h * n_lo + lo - e, m, wait_send)

                @pl.when(lo + e < n_lo)
                def _():
                    each_way((3,), h * n_lo + lo + e, m, wait_send)

    def sent(j, carry):
        @pl.when(j != q)
        def _():
            a_copy(j).wait_send()
            n_copy(j).wait_send()

        return carry

    lax.fori_loop(0, n_seq, sent, 0)


def shards(sections, n_seq, base_ids, stem_weight, conv_weight, block_gain, cotangent):
    micro, rows, chans = cotangent.shape
    n_lo = max(1, n_seq // 4)
    halo = -(-4 * (sections - 1) // 16) * 16
    ext = rows + 2 * halo
    e_halo = halo + 16
    part = chans // n_seq
    taps = STEM_K * BASES
    lane = jnp.arange(LANES, dtype=jnp.int32)
    wanted = jnp.where(lane < taps, lane % BASES, -1)
    spread = (base_ids[:, :, None] == wanted).astype(F32)
    stem = jnp.pad(stem_weight.reshape(taps, chans), ((0, LANES - taps), (0, 0)))
    vmem, dma = pltpu.VMEM, pltpu.SemaphoreType.DMA
    flow = vmem((micro, ext, chans), BF16)
    scratch = [
        vmem((micro, rows + 2 * e_halo, LANES), F32),
        vmem((micro, ext, chans), F32),
        vmem((micro, ext + 2 * EDGE, chans), F32),
        vmem((ext, KERNEL * chans), BF16),
        vmem((micro, ext + 2 * EDGE, chans), F32),
        vmem((micro, ext, chans), F32),
        flow, flow, flow, flow, flow, flow,
        vmem((2, micro, halo, chans), BF16),
        vmem((n_seq, micro, rows, LANES), BF16),
        vmem((n_seq, micro, rows, LANES), BF16),
        vmem((micro, n_seq * rows + 2 * EDGE, LANES), F32),
        vmem((n_seq, KERNEL * LANES, micro * rows), BF16),
        vmem((n_seq, micro, rows, chans), BF16),
        vmem((KERNEL * LANES, chans), F32),
        vmem((8, chans), F32),
        vmem((n_seq, 8, LANES), F32),
        vmem((n_seq, 8, LANES), F32),
        dma((2,)), dma((2,)), dma((2,)), dma((2,)),
        dma((micro, 2)), dma((micro, 2)), dma((micro, 2)), dma((micro, 2)),
        dma((n_seq,)), dma((n_seq,)), dma((n_seq,)), dma((n_seq,)),
        dma((n_seq, micro, 4)), dma((n_seq, micro)),
    ]
    conv_grad, gain_grad = pl.pallas_call(
        functools.partial(level_kernel, sections, n_seq, n_lo, micro, rows, chans, halo),
        out_shape=(
            jax.ShapeDtypeStruct((KERNEL, part, chans), BF16),
            jax.ShapeDtypeStruct((1, part), F32),
        ),
        in_specs=[pl.BlockSpec(memory_space=pltpu.VMEM)] * 5,
        out_specs=(pl.BlockSpec(memory_space=pltpu.VMEM),) * 2,
        scratch_shapes=scratch,
        compiler_params=pltpu.CompilerParams(
            collective_id=0, has_side_effects=True, vmem_limit_bytes=58 * 2**20
        ),
    )(spread, stem, conv_weight[0].reshape(KERNEL * chans, chans), block_gain, cotangent)
    return conv_grad[None], gain_grad


def solution(mesh):
    placed = (
        P(None, "seq"),
        P(),
        P("section", None, None, None),
        P("section", None),
        P(None, "seq", None),
    )
    return jax.shard_map(
        functools.partial(shards, mesh.shape["section"], mesh.shape["seq"]),
        mesh=mesh,
        in_specs=placed,
        out_specs=(P("section", None, "seq", None), P("section", "seq")),
        check_vma=False,
    )
```

```python
import functools

import jax
import jax.numpy as jnp
from jax import lax
from jax.experimental import pallas as pl
from jax.experimental.pallas import tpu as pltpu
from jax.sharding import PartitionSpec as P

KERNEL = 5
STEM_K = 15
BASES = 4
LANES = 128
EDGE = 8
F32, BF16 = jnp.float32, jnp.bfloat16
GELU_A, GELU_B = 0.7978845608028654, 0.044715


def remote(src, dst, send_sem, recv_sem, **where):
    return pltpu.make_async_remote_copy(
        src_ref=src,
        dst_ref=dst,
        send_sem=send_sem,
        recv_sem=recv_sem,
        device_id=where,
        device_id_type=pl.DeviceIdType.MESH,
    )


def level_kernel(
    sections, n_seq, n_lo, micro, rows, chans, halo,
    ids_ref, stem_ref, w_hbm, gain_ref, cot_ref,
    out_ref, gout_ref,
    w_ref, stemf, ebuf, bsum, actf, x5, gradf, gact, inflow, skip, fout, gin, gskip, gsend, coth,
    aslab, acol, acolf, a5t, gall, acc, gain_acc, gslab, grecv,
    e_send, e_recv, c_send, c_recv, f_send, f_recv, b_send, b_recv,
    a_send, a_recv, n_send, n_recv, ag_send, ag_recv, w_sem,
):
    sec, q = lax.axis_index("section"), lax.axis_index("seq")
    n_hi = n_seq // n_lo
    hi, lo = q // n_lo, q % n_lo
    half = sections // 2
    ext = rows + 2 * halo
    e_halo = halo + 16
    part = chans // n_seq
    reach = (KERNEL - 1) // 2
    last = sections - 1
    mirror_sec = last - sec
    step = 32
    tokens = rows * n_seq

    w_copy = pltpu.make_async_copy(w_hbm, w_ref, w_sem)
    w_copy.start()
    barrier = pltpu.get_barrier_semaphore()
    for d in range(1, n_seq):
        pl.semaphore_signal(
            barrier, inc=1, device_id={"seq": (q + d) % n_seq}, device_id_type=pl.DeviceIdType.MESH
        )
    for d in range(1, sections):
        pl.semaphore_signal(
            barrier, inc=1, device_id={"section": (sec + d) % sections},
            device_id_type=pl.DeviceIdType.MESH,
        )
    pl.semaphore_wait(barrier, n_seq + sections - 2)

    def e_copy(side):
        if side == 0:
            src, dst, to = ebuf.at[:, rows : e_halo + rows], ebuf.at[:, 0:e_halo], q + 1
        else:
            src, dst, to = ebuf.at[:, e_halo : 2 * e_halo], ebuf.at[:, e_halo + rows :], q - 1
        return remote(src, dst, e_send.at[side], e_recv.at[side], seq=to)

    def c_copy(side):
        if side == 0:
            src, dst, to = cot_ref.at[:, rows - halo : rows], coth.at[0], q + 1
        else:
            src, dst, to = cot_ref.at[:, 0:halo], coth.at[1], q - 1
        return remote(src, dst, c_send.at[side], c_recv.at[side], seq=to)

    def gather_copy(block, m, way):
        to = [q + n_lo, q - n_lo, q + 1, q - 1][way]
        return remote(
            gall.at[block, m], gall.at[block, m], ag_send.at[block, m, way],
            ag_recv.at[block, m], seq=to,
        )

    up, down, right, left = hi < n_hi - 1, hi > 0, lo < n_lo - 1, lo > 0

    def each_way(ways, block, m, act):
        for way in ways:
            @pl.when([up, down, right, left][way])
            def _():
                act(gather_copy(block, m, way))

    def start(copy):
        copy.start()

    def wait_send(copy):
        copy.wait_send()

    for ref in (actf, gradf):
        ref[:, 0:EDGE] = jnp.zeros((micro, EDGE, chans), F32)
        ref[:, EDGE + ext :] = jnp.zeros((micro, EDGE, chans), F32)
    acolf[:, 0:EDGE] = jnp.zeros((micro, EDGE, LANES), F32)
    acolf[:, EDGE + tokens :] = jnp.zeros((micro, EDGE, LANES), F32)
    gain_acc[...] = jnp.zeros_like(gain_acc)
    acc[...] = jnp.zeros_like(acc)

    @pl.when(sec == 0)
    def _():
        lane = lax.broadcasted_iota(jnp.int32, (rows, LANES), 1)
        wanted = jnp.where(lane < STEM_K * BASES, lane % BASES, -1).astype(F32)
        for m in range(micro):
            ids = jnp.broadcast_to(ids_ref[m : m + 1, :].astype(F32), (LANES, rows)).T
            ebuf[m, e_halo : e_halo + rows] = jnp.where(ids == wanted, 1.0, 0.0)

        @pl.when(q < n_seq - 1)
        def _():
            e_copy(0).start()

        @pl.when(q > 0)
        def _():
            e_copy(1).start()

        stemf[...] = jnp.zeros_like(stemf)
        for k in range(STEM_K):
            stemf[k * BASES : (k + 1) * BASES] = stem_ref[k].astype(F32)

        @pl.when(q == 0)
        def _():
            ebuf[:, 0:e_halo] = jnp.zeros((micro, e_halo, LANES), F32)

        @pl.when(q == n_seq - 1)
        def _():
            ebuf[:, e_halo + rows :] = jnp.zeros((micro, e_halo, LANES), F32)

        @pl.when(q > 0)
        def _():
            e_copy(0).wait_recv()

        @pl.when(q < n_seq - 1)
        def _():
            e_copy(1).wait_recv()

    def row_mask(first, count):
        place = lax.broadcasted_iota(jnp.int32, (count, 1), 0) + (first + q * rows - halo)
        return (place >= 0) & (place < tokens)

    def shifted(ref, m, flip):
        for k in range(KERNEL):
            off = EDGE + (reach - k if flip else k - reach)
            x5[:, k * chans : (k + 1) * chans] = ref[m, off : off + ext].astype(BF16)

    def conv_back(m):
        shifted(gradf, m, True)

        def tile(n, carry):
            at = pl.ds(pl.multiple_of(n * 256, 256), 256)
            total = jnp.zeros((ext, 256), F32)
            for k in range(KERNEL):
                total = total + lax.dot_general(
                    x5[:, k * chans : (k + 1) * chans],
                    w_ref[pl.ds(pl.multiple_of(k * chans + n * 256, 256), 256), :],
                    (((1,), (1,)), ((), ())),
                    preferred_element_type=F32,
                )
            gact[m, :, at] = total
            return carry

        lax.fori_loop(0, chans // 256, tile, 0)

    def multiply(block):
        def tile(n, c):
            at = pl.ds(pl.multiple_of(n * 256, 256), 256)
            acc[:, at] += jnp.dot(
                a5t[block], gall[block, :, :, at].reshape(micro * rows, 256),
                preferred_element_type=F32,
            )
            return c

        lax.fori_loop(0, chans // 256, tile, 0)

    def gather(then):
        then(q)
        for d in range(1, n_hi):
            for m in range(micro):
                @pl.when(hi - d >= 0)
                def _():
                    gather_copy(q - d * n_lo, m, 0).wait_recv()
                    each_way((0, 2, 3), q - d * n_lo, m, start)

                @pl.when(hi + d < n_hi)
                def _():
                    gather_copy(q + d * n_lo, m, 1).wait_recv()
                    each_way((1, 2, 3), q + d * n_lo, m, start)

            @pl.when(hi - d >= 0)
            def _():
                then(q - d * n_lo)

            @pl.when(hi + d < n_hi)
            def _():
                then(q + d * n_lo)

        for e in range(1, n_lo):
            for d in range(n_hi):
                for side in (-1, 1) if d else (1,):
                    h = hi + side * d

                    @pl.when((h >= 0) & (h < n_hi) & (lo - e >= 0))
                    def _():
                        block = h * n_lo + lo - e
                        for m in range(micro):
                            gather_copy(block, m, 2).wait_recv()
                            each_way((2,), block, m, start)
                        then(block)

                    @pl.when((h >= 0) & (h < n_hi) & (lo + e < n_lo))
                    def _():
                        block = h * n_lo + lo + e
                        for m in range(micro):
                            gather_copy(block, m, 3).wait_recv()
                            each_way((3,), block, m, start)
                        then(block)

    @pl.when(sec == last)
    def _():
        @pl.when(q < n_seq - 1)
        def _():
            c_copy(0).start()

        @pl.when(q > 0)
        def _():
            c_copy(1).start()

        gall[q] = cot_ref[...]
        for m in range(micro):
            each_way(range(4), q, m, start)
        gradf[:, EDGE + halo : EDGE + halo + rows] = cot_ref[...].astype(F32)

        @pl.when(q == 0)
        def _():
            gradf[:, EDGE : EDGE + halo] = jnp.zeros((micro, halo, chans), F32)

        @pl.when(q == n_seq - 1)
        def _():
            gradf[:, EDGE + halo + rows : EDGE + ext] = jnp.zeros((micro, halo, chans), F32)

        @pl.when(q > 0)
        def _():
            c_copy(0).wait_recv()
            gradf[:, EDGE : EDGE + halo] = coth[0].astype(F32)

        @pl.when(q < n_seq - 1)
        def _():
            c_copy(1).wait_recv()
            gradf[:, EDGE + halo + rows : EDGE + ext] = coth[1].astype(F32)

        w_copy.wait()

        def each(m, carry):
            conv_back(m)
            return carry

        lax.fori_loop(0, micro, each, 0)
        gather(lambda block: None)

    def f_copy(m, kind):
        to = sec + 1 if kind == 0 else mirror_sec
        dst = inflow if kind == 0 else skip
        return remote(fout.at[m], dst.at[m], f_send.at[m, kind], f_recv.at[m, kind], section=to)

    def b_copy(m, kind):
        to = sec - 1 if kind == 0 else mirror_sec
        dst = gin if kind == 0 else gskip
        return remote(gsend.at[m], dst.at[m], b_send.at[m, kind], b_recv.at[m, kind], section=to)

    def by_rows(body):
        def one(i, carry):
            body(pl.multiple_of(i * step, step))
            return carry

        lax.fori_loop(0, ext // step, one, 0)

    def forward(m, carry):
        @pl.when(sec == 0)
        def _():
            tap = lax.broadcasted_iota(jnp.int32, (ext, LANES), 1) // BASES
            hot = jnp.zeros((ext, LANES), F32)
            for k in range(STEM_K):
                off = e_halo - halo + k - (STEM_K - 1) // 2
                hot = jnp.where(tap == k, ebuf[m, off : off + ext], hot)
            stem = jnp.dot(
                hot.astype(BF16), stemf[...].astype(BF16), preferred_element_type=F32
            )
            bsum[m] = stem.astype(BF16).astype(F32)

        @pl.when(sec > 0)
        def _():
            f_copy(m, 0).wait_recv()

            @pl.when(sec < half)
            def _():
                bsum[m] = inflow[m].astype(F32)

            @pl.when(sec == half)
            def _():
                bsum[m] = inflow[m].astype(F32) * 2.0

            @pl.when(sec > half)
            def _():
                f_copy(m, 1).wait_recv()
                bsum[m] = inflow[m].astype(F32) + skip[m].astype(F32)

        def act_rows(r):
            b = bsum[m, pl.ds(r, step)]
            scale = lax.rsqrt(jnp.mean(b * b, axis=-1, keepdims=True) + 1e-06)
            x = b * scale * gain_ref[...]
            t = jnp.tanh(GELU_A * (x + GELU_B * (x * x * x)))
            y = (x * (0.5 * (1.0 + t))).astype(BF16).astype(F32)
            actf[m, pl.ds(pl.multiple_of(EDGE + r, 8), step)] = jnp.where(row_mask(r, step), y, 0.0)

        by_rows(act_rows)

        @pl.when(sec < last)
        def _():
            shifted(actf, m, False)

            @pl.when(m == 0)
            def _():
                w_copy.wait()

            def tile(n, c):
                at = pl.ds(pl.multiple_of(n * 256, 256), 256)
                total = bsum[m, :, at] + jnp.dot(
                    x5[...], w_ref[:, at], preferred_element_type=F32
                )
                fout[m, :, at] = total.astype(BF16)
                return c

            lax.fori_loop(0, chans // 256, tile, 0)
            f_copy(m, 0).start()

            @pl.when(sec < half - 1)
            def _():
                f_copy(m, 1).start()

        return carry

    lax.fori_loop(0, micro, forward, 0)

    def picker(j):
        c = lax.broadcasted_iota(jnp.int32, (chans, LANES), 0)
        lane = lax.broadcasted_iota(jnp.int32, (chans, LANES), 1)
        return jnp.where((c == j * part + lane) & (lane < part), 1.0, 0.0).astype(BF16)

    def a_copy(j):
        return remote(aslab.at[j], acol.at[q], a_send.at[j], a_recv.at[q], seq=j)

    def a_from(j):
        return remote(aslab.at[j], acol.at[j], a_send.at[j], a_recv.at[j], seq=j)

    def spread_rows():
        own = slice(EDGE + halo, EDGE + halo + rows)

        def slab(j, carry):
            pick = picker(j)
            for m in range(micro):
                aslab[j, m] = jnp.dot(
                    actf[m, own].astype(BF16), pick, preferred_element_type=F32
                ).astype(BF16)

            @pl.when(j != q)
            def _():
                a_copy(j).start()

            @pl.when(j == q)
            def _():
                acol[j] = aslab[j]

            return carry

        lax.fori_loop(0, n_seq, slab, 0)

        def take(j, carry):
            @pl.when(j != q)
            def _():
                a_from(j).wait_recv()

            at = pl.ds(pl.multiple_of(EDGE + j * rows, 8), rows)
            for m in range(micro):
                acolf[m, at] = acol[j, m].astype(F32)
            return carry

        lax.fori_loop(0, n_seq, take, 0)

        def turn(j, carry):
            for m in range(micro):
                window = acolf[m, pl.ds(pl.multiple_of(j * rows, rows), rows + 2 * EDGE)]
                for k in range(KERNEL):
                    off = EDGE + k - reach
                    a5t[j, k * LANES : (k + 1) * LANES, m * rows : (m + 1) * rows] = (
                        window[off : off + rows].T.astype(BF16)
                    )
            return carry

        lax.fori_loop(0, n_seq, turn, 0)

    @pl.when(sec < half)
    def _():
        spread_rows()

    def backward(m, carry):
        @pl.when(sec < last)
        def _():
            b_copy(m, 0).wait_recv()

            @pl.when(sec < half - 1)
            def _():
                b_copy(m, 1).wait_recv()
                gradf[m, EDGE : EDGE + ext] = (
                    (gin[m].astype(F32) + gskip[m].astype(F32)).astype(BF16).astype(F32)
                )

            @pl.when(sec == half - 1)
            def _():
                gradf[m, EDGE : EDGE + ext] = gin[m].astype(F32) * 2.0

            @pl.when(sec >= half)
            def _():
                gradf[m, EDGE : EDGE + ext] = gin[m].astype(F32)

            gall[q, m] = gradf[m, EDGE + halo : EDGE + halo + rows].astype(BF16)
            each_way(range(4), q, m, start)
            conv_back(m)

        def pull_rows(r):
            at = pl.ds(r, step)
            b, grad = bsum[m, at], gact[m, at]
            scale = lax.rsqrt(jnp.mean(b * b, axis=-1, keepdims=True) + 1e-06)
            unit = b * scale
            x = unit * gain_ref[...]
            t = jnp.tanh(GELU_A * (x + GELU_B * (x * x * x)))
            slope = 0.5 * (1.0 + t) + (0.5 * GELU_A) * x * (1.0 - t * t) * (
                1.0 + (3.0 * GELU_B) * (x * x)
            )
            d_pre = grad * slope
            d_unit = d_pre * gain_ref[...]
            place = lax.broadcasted_iota(jnp.int32, (step, 1), 0) + r
            mine = (place >= halo) & (place < halo + rows)
            terms = jnp.where(mine, d_pre * unit, 0.0)
            gain_acc[...] += jnp.sum(terms.reshape(step // 8, 8, chans), axis=0)
            pulled = scale * (d_unit - unit * jnp.mean(d_unit * unit, axis=-1, keepdims=True))
            whole = gradf[m, pl.ds(pl.multiple_of(EDGE + r, 8), step)] + pulled
            gsend[m, at] = jnp.where(row_mask(r, step), whole, 0.0).astype(BF16)

        by_rows(pull_rows)

        @pl.when(sec > 0)
        def _():
            b_copy(m, 0).start()

            @pl.when(sec > half)
            def _():
                b_copy(m, 1).start()

        return carry

    lax.fori_loop(0, micro, backward, 0)

    @pl.when((sec >= half) & (sec < last))
    def _():
        gather(lambda block: None)

    @pl.when(sec >= half)
    def _():
        spread_rows()

    def n_copy(j):
        return remote(gslab.at[j], grecv.at[q], n_send.at[j], n_recv.at[q], seq=j)

    def n_from(j):
        return remote(gslab.at[j], grecv.at[j], n_send.at[j], n_recv.at[j], seq=j)

    gain_part = jnp.broadcast_to(jnp.sum(gain_acc[...], axis=0, keepdims=True), (16, chans))
    gain_part = gain_part.astype(BF16)

    def gain_slab(j, carry):
        gslab[j] = jnp.dot(gain_part, picker(j), preferred_element_type=F32)[0:8]

        @pl.when(j != q)
        def _():
            n_copy(j).start()

        @pl.when(j == q)
        def _():
            grecv[j] = gslab[j]

        return carry

    lax.fori_loop(0, n_seq, gain_slab, 0)

    @pl.when(sec < half)
    def _():
        gather(multiply)

    @pl.when(sec >= half)
    def _():
        def one(j, carry):
            multiply(j)
            return carry

        lax.fori_loop(0, n_seq, one, 0)

    for k in range(KERNEL):
        out_ref[k] = acc[k * LANES : k * LANES + part].astype(BF16)

    def gain_take(j, total):
        @pl.when(j != q)
        def _():
            n_from(j).wait_recv()

        return total + grecv[j]

    gain_total = lax.fori_loop(0, n_seq, gain_take, jnp.zeros((8, LANES), F32))
    gout_ref[...] = gain_total[0:1, 0:part]

    @pl.when(sec == 0)
    def _():
        @pl.when(q < n_seq - 1)
        def _():
            e_copy(0).wait_send()

        @pl.when(q > 0)
        def _():
            e_copy(1).wait_send()

    @pl.when(sec == last)
    def _():
        @pl.when(q < n_seq - 1)
        def _():
            c_copy(0).wait_send()

        @pl.when(q > 0)
        def _():
            c_copy(1).wait_send()

    for m in range(micro):
        @pl.when(sec < last)
        def _():
            f_copy(m, 0).wait_send()

        @pl.when(sec < half - 1)
        def _():
            f_copy(m, 1).wait_send()

        @pl.when(sec > 0)
        def _():
            b_copy(m, 0).wait_send()

        @pl.when(sec > half)
        def _():
            b_copy(m, 1).wait_send()

        each_way(range(4), q, m, wait_send)
        for d in range(1, n_hi):
            @pl.when(hi - d >= 0)
            def _():
                each_way((0, 2, 3), q - d * n_lo, m, wait_send)

            @pl.when(hi + d < n_hi)
            def _():
                each_way((1, 2, 3), q + d * n_lo, m, wait_send)

        for e in range(1, n_lo):
            for h in range(n_hi):
                @pl.when(lo - e >= 0)
                def _():
                    each_way((2,), h * n_lo + lo - e, m, wait_send)

                @pl.when(lo + e < n_lo)
                def _():
                    each_way((3,), h * n_lo + lo + e, m, wait_send)

    def sent(j, carry):
        @pl.when(j != q)
        def _():
            a_copy(j).wait_send()
            n_copy(j).wait_send()

        return carry

    lax.fori_loop(0, n_seq, sent, 0)


def finish(conv_ref, gain_ref, out_ref, gout_ref):
    out_ref[0] = conv_ref[...]
    gout_ref[...] = gain_ref[...]


def shards(sections, n_seq, base_ids, stem_weight, conv_weight, block_gain, cotangent):
    micro, rows, chans = cotangent.shape
    n_lo = max(1, n_seq // 4)
    halo = -(-4 * (sections - 1) // 16) * 16
    ext = rows + 2 * halo
    e_halo = halo + 16
    part = chans // n_seq
    vmem, dma = pltpu.VMEM, pltpu.SemaphoreType.DMA
    flow = vmem((micro, ext, chans), BF16)
    scratch = [
        vmem((KERNEL * chans, chans), BF16),
        vmem((LANES, chans), F32),
        vmem((micro, rows + 2 * e_halo, LANES), F32),
        vmem((micro, ext, chans), F32),
        vmem((micro, ext + 2 * EDGE, chans), F32),
        vmem((ext, KERNEL * chans), BF16),
        vmem((micro, ext + 2 * EDGE, chans), F32),
        vmem((micro, ext, chans), F32),
        flow, flow, flow, flow, flow, flow,
        vmem((2, micro, halo, chans), BF16),
        vmem((n_seq, micro, rows, LANES), BF16),
        vmem((n_seq, micro, rows, LANES), BF16),
        vmem((micro, n_seq * rows + 2 * EDGE, LANES), F32),
        vmem((n_seq, KERNEL * LANES, micro * rows), BF16),
        vmem((n_seq, micro, rows, chans), BF16),
        vmem((KERNEL * LANES, chans), F32),
        vmem((8, chans), F32),
        vmem((n_seq, 8, LANES), F32),
        vmem((n_seq, 8, LANES), F32),
        dma((2,)), dma((2,)), dma((2,)), dma((2,)),
        dma((micro, 2)), dma((micro, 2)), dma((micro, 2)), dma((micro, 2)),
        dma((n_seq,)), dma((n_seq,)), dma((n_seq,)), dma((n_seq,)),
        dma((n_seq, micro, 4)), dma((n_seq, micro)), dma,
    ]
    conv_grad, gain_grad = pl.pallas_call(
        functools.partial(level_kernel, sections, n_seq, n_lo, micro, rows, chans, halo),
        out_shape=(
            jax.ShapeDtypeStruct((KERNEL, part, chans), BF16),
            jax.ShapeDtypeStruct((1, part), F32),
        ),
        in_specs=[pl.BlockSpec(memory_space=pl.ANY if i == 2 else vmem) for i in range(5)],
        out_specs=(pl.BlockSpec(memory_space=pltpu.VMEM),) * 2,
        scratch_shapes=scratch,
        compiler_params=pltpu.CompilerParams(
            collective_id=0, has_side_effects=True, vmem_limit_bytes=58 * 2**20
        ),
    )(base_ids, stem_weight, conv_weight[0].reshape(KERNEL * chans, chans), block_gain, cotangent)
    whole = pl.BlockSpec(memory_space=vmem)
    conv_grad, gain_grad = pl.pallas_call(
        finish,
        out_shape=(
            jax.ShapeDtypeStruct((1, KERNEL, part, chans), BF16),
            jax.ShapeDtypeStruct((1, part), F32),
        ),
        in_specs=[whole, whole],
        out_specs=(whole, whole),
    )(conv_grad, gain_grad)
    return conv_grad, gain_grad


def solution(mesh):
    placed = (
        P(None, "seq"),
        P(),
        P("section", None, None, None),
        P("section", None),
        P(None, "seq", None),
    )
    return jax.shard_map(
        functools.partial(shards, mesh.shape["section"], mesh.shape["seq"]),
        mesh=mesh,
        in_specs=placed,
        out_specs=(P("section", None, "seq", None), P("section", "seq")),
        check_vma=False,
    )
```

```python
import functools

import jax
import jax.numpy as jnp
from jax import lax
from jax.experimental import pallas as pl
from jax.experimental.pallas import tpu as pltpu
from jax.sharding import PartitionSpec as P

KERNEL = 5
STEM_K = 15
BASES = 4
LANES = 128
EDGE = 8
F32, BF16 = jnp.float32, jnp.bfloat16
GELU_A, GELU_B = 0.7978845608028654, 0.044715


def remote(src, dst, send_sem, recv_sem, **where):
    return pltpu.make_async_remote_copy(
        src_ref=src,
        dst_ref=dst,
        send_sem=send_sem,
        recv_sem=recv_sem,
        device_id=where,
        device_id_type=pl.DeviceIdType.MESH,
    )


def level_kernel(
    sections, n_seq, n_lo, micro, rows, chans, halo,
    ids_ref, stem_ref, w_hbm, gain_ref, cot_ref,
    out_ref, gout_ref,
    w_ref, stemf, ebuf, bsum, actf, x5, gradf, gact, inflow, skip, fout, gin, gskip, gsend, coth,
    aslab, acol, acolf, a5t, gall, acc, gain_acc, gslab, grecv,
    e_send, e_recv, c_send, c_recv, f_send, f_recv, b_send, b_recv,
    a_send, a_recv, n_send, n_recv, ag_send, ag_recv, w_sem,
):
    sec, q = lax.axis_index("section"), lax.axis_index("seq")
    n_hi = n_seq // n_lo
    hi, lo = q // n_lo, q % n_lo
    half = sections // 2
    ext = rows + 2 * halo
    e_halo = halo + 16
    part = chans // n_seq
    reach = (KERNEL - 1) // 2
    last = sections - 1
    mirror_sec = last - sec
    step = 32
    tokens = rows * n_seq

    w_copy = pltpu.make_async_copy(w_hbm, w_ref, w_sem)
    w_copy.start()
    barrier = pltpu.get_barrier_semaphore()
    for d in range(1, n_seq):
        pl.semaphore_signal(
            barrier, inc=1, device_id={"seq": (q + d) % n_seq}, device_id_type=pl.DeviceIdType.MESH
        )
    for d in range(1, sections):
        pl.semaphore_signal(
            barrier, inc=1, device_id={"section": (sec + d) % sections},
            device_id_type=pl.DeviceIdType.MESH,
        )
    pl.semaphore_wait(barrier, n_seq + sections - 2)

    def e_copy(side):
        if side == 0:
            src, dst, to = ebuf.at[:, rows : e_halo + rows], ebuf.at[:, 0:e_halo], q + 1
        else:
            src, dst, to = ebuf.at[:, e_halo : 2 * e_halo], ebuf.at[:, e_halo + rows :], q - 1
        return remote(src, dst, e_send.at[side], e_recv.at[side], seq=to)

    def c_copy(side):
        if side == 0:
            src, dst, to = cot_ref.at[:, rows - halo : rows], coth.at[0], q + 1
        else:
            src, dst, to = cot_ref.at[:, 0:halo], coth.at[1], q - 1
        return remote(src, dst, c_send.at[side], c_recv.at[side], seq=to)

    def gather_copy(block, m, way):
        to = [q + n_lo, q - n_lo, q + 1, q - 1][way]
        return remote(
            gall.at[block, m], gall.at[block, m], ag_send.at[block, m, way],
            ag_recv.at[block, m], seq=to,
        )

    up, down, right, left = hi < n_hi - 1, hi > 0, lo < n_lo - 1, lo > 0

    def each_way(ways, block, m, act):
        for way in ways:
            @pl.when([up, down, right, left][way])
            def _():
                act(gather_copy(block, m, way))

    def start(copy):
        copy.start()

    def wait_send(copy):
        copy.wait_send()

    for ref in (actf, gradf):
        ref[:, 0:EDGE] = jnp.zeros((micro, EDGE, chans), F32)
        ref[:, EDGE + ext :] = jnp.zeros((micro, EDGE, chans), F32)
    acolf[:, 0:EDGE] = jnp.zeros((micro, EDGE, LANES), F32)
    acolf[:, EDGE + tokens :] = jnp.zeros((micro, EDGE, LANES), F32)
    gain_acc[...] = jnp.zeros_like(gain_acc)
    acc[...] = jnp.zeros_like(acc)

    @pl.when(sec == 0)
    def _():
        lane = lax.broadcasted_iota(jnp.int32, (rows, LANES), 1)
        wanted = jnp.where(lane < STEM_K * BASES, lane % BASES, -1).astype(F32)
        for m in range(micro):
            ids = jnp.broadcast_to(ids_ref[m : m + 1, :].astype(F32), (LANES, rows)).T
            ebuf[m, e_halo : e_halo + rows] = jnp.where(ids == wanted, 1.0, 0.0)

        @pl.when(q < n_seq - 1)
        def _():
            e_copy(0).start()

        @pl.when(q > 0)
        def _():
            e_copy(1).start()

        stemf[...] = jnp.zeros_like(stemf)
        for k in range(STEM_K):
            stemf[k * BASES : (k + 1) * BASES] = stem_ref[k].astype(F32)

        @pl.when(q == 0)
        def _():
            ebuf[:, 0:e_halo] = jnp.zeros((micro, e_halo, LANES), F32)

        @pl.when(q == n_seq - 1)
        def _():
            ebuf[:, e_halo + rows :] = jnp.zeros((micro, e_halo, LANES), F32)

        @pl.when(q > 0)
        def _():
            e_copy(0).wait_recv()

        @pl.when(q < n_seq - 1)
        def _():
            e_copy(1).wait_recv()

    def row_mask(first, count):
        place = lax.broadcasted_iota(jnp.int32, (count, 1), 0) + (first + q * rows - halo)
        return (place >= 0) & (place < tokens)

    def shifted(ref, m, flip):
        for k in range(KERNEL):
            off = EDGE + (reach - k if flip else k - reach)
            x5[:, k * chans : (k + 1) * chans] = ref[m, off : off + ext].astype(BF16)

    def conv_back(m):
        shifted(gradf, m, True)

        def tile(n, carry):
            at = pl.ds(pl.multiple_of(n * 256, 256), 256)
            total = jnp.zeros((ext, 256), F32)
            for k in range(KERNEL):
                total = total + lax.dot_general(
                    x5[:, k * chans : (k + 1) * chans],
                    w_ref[pl.ds(pl.multiple_of(k * chans + n * 256, 256), 256), :],
                    (((1,), (1,)), ((), ())),
                    preferred_element_type=F32,
                )
            gact[m, :, at] = total
            return carry

        lax.fori_loop(0, chans // 256, tile, 0)

    def multiply(block):
        def tile(n, c):
            at = pl.ds(pl.multiple_of(n * 256, 256), 256)
            acc[:, at] += jnp.dot(
                a5t[block], gall[block, :, :, at].reshape(micro * rows, 256),
                preferred_element_type=F32,
            )
            return c

        lax.fori_loop(0, chans // 256, tile, 0)

    def gather_column(then):
        then(q)
        for d in range(1, n_hi):
            for m in range(micro):
                @pl.when(hi - d >= 0)
                def _():
                    gather_copy(q - d * n_lo, m, 0).wait_recv()
                    each_way((0, 2, 3), q - d * n_lo, m, start)

                @pl.when(hi + d < n_hi)
                def _():
                    gather_copy(q + d * n_lo, m, 1).wait_recv()
                    each_way((1, 2, 3), q + d * n_lo, m, start)

            @pl.when(hi - d >= 0)
            def _():
                then(q - d * n_lo)

            @pl.when(hi + d < n_hi)
            def _():
                then(q + d * n_lo)

    def gather_row(then):
        for e in range(1, n_lo):
            for d in range(n_hi):
                for side in (-1, 1) if d else (1,):
                    h = hi + side * d

                    @pl.when((h >= 0) & (h < n_hi) & (lo - e >= 0))
                    def _():
                        block = h * n_lo + lo - e
                        for m in range(micro):
                            gather_copy(block, m, 2).wait_recv()
                            each_way((2,), block, m, start)
                        then(block)

                    @pl.when((h >= 0) & (h < n_hi) & (lo + e < n_lo))
                    def _():
                        block = h * n_lo + lo + e
                        for m in range(micro):
                            gather_copy(block, m, 3).wait_recv()
                            each_way((3,), block, m, start)
                        then(block)

    @pl.when(sec == last)
    def _():
        @pl.when(q < n_seq - 1)
        def _():
            c_copy(0).start()

        @pl.when(q > 0)
        def _():
            c_copy(1).start()

        gall[q] = cot_ref[...]
        for m in range(micro):
            each_way(range(4), q, m, start)
        gradf[:, EDGE + halo : EDGE + halo + rows] = cot_ref[...].astype(F32)

        @pl.when(q == 0)
        def _():
            gradf[:, EDGE : EDGE + halo] = jnp.zeros((micro, halo, chans), F32)

        @pl.when(q == n_seq - 1)
        def _():
            gradf[:, EDGE + halo + rows : EDGE + ext] = jnp.zeros((micro, halo, chans), F32)

        @pl.when(q > 0)
        def _():
            c_copy(0).wait_recv()
            gradf[:, EDGE : EDGE + halo] = coth[0].astype(F32)

        @pl.when(q < n_seq - 1)
        def _():
            c_copy(1).wait_recv()
            gradf[:, EDGE + halo + rows : EDGE + ext] = coth[1].astype(F32)

        w_copy.wait()

        def each(m, carry):
            conv_back(m)
            return carry

        lax.fori_loop(0, micro, each, 0)
        gather_column(lambda block: None)

    def f_copy(m, kind):
        to = sec + 1 if kind == 0 else mirror_sec
        dst = inflow if kind == 0 else skip
        return remote(fout.at[m], dst.at[m], f_send.at[m, kind], f_recv.at[m, kind], section=to)

    def b_copy(m, kind):
        to = sec - 1 if kind == 0 else mirror_sec
        dst = gin if kind == 0 else gskip
        return remote(gsend.at[m], dst.at[m], b_send.at[m, kind], b_recv.at[m, kind], section=to)

    def by_rows(body):
        def one(i, carry):
            body(pl.multiple_of(i * step, step))
            return carry

        lax.fori_loop(0, ext // step, one, 0, unroll=True)

    def pull_back(m):
        def pull_rows(r):
            at = pl.ds(r, step)
            b, grad = bsum[m, at], gact[m, at]
            scale = lax.rsqrt(jnp.mean(b * b, axis=-1, keepdims=True) + 1e-06)
            unit = b * scale
            x = unit * gain_ref[...]
            t = jnp.tanh(GELU_A * (x + GELU_B * (x * x * x)))
            slope = 0.5 * (1.0 + t) + (0.5 * GELU_A) * x * (1.0 - t * t) * (
                1.0 + (3.0 * GELU_B) * (x * x)
            )
            d_pre = grad * slope
            d_unit = d_pre * gain_ref[...]
            place = lax.broadcasted_iota(jnp.int32, (step, 1), 0) + r
            mine = (place >= halo) & (place < halo + rows)
            terms = jnp.where(mine, d_pre * unit, 0.0)
            gain_acc[...] += jnp.sum(terms.reshape(step // 8, 8, chans), axis=0)
            pulled = scale * (d_unit - unit * jnp.mean(d_unit * unit, axis=-1, keepdims=True))
            whole = gradf[m, pl.ds(pl.multiple_of(EDGE + r, 8), step)] + pulled
            gsend[m, at] = jnp.where(row_mask(r, step), whole, 0.0).astype(BF16)

        by_rows(pull_rows)

        @pl.when(sec > 0)
        def _():
            b_copy(m, 0).start()

            @pl.when(sec > half)
            def _():
                b_copy(m, 1).start()


    def forward(m, carry):
        @pl.when(sec == 0)
        def _():
            tap = lax.broadcasted_iota(jnp.int32, (ext, LANES), 1) // BASES
            hot = jnp.zeros((ext, LANES), F32)
            for k in range(STEM_K):
                off = e_halo - halo + k - (STEM_K - 1) // 2
                hot = jnp.where(tap == k, ebuf[m, off : off + ext], hot)
            stem = jnp.dot(
                hot.astype(BF16), stemf[...].astype(BF16), preferred_element_type=F32
            )
            bsum[m] = stem.astype(BF16).astype(F32)

        @pl.when(sec > 0)
        def _():
            f_copy(m, 0).wait_recv()

            @pl.when(sec < half)
            def _():
                bsum[m] = inflow[m].astype(F32)

            @pl.when(sec == half)
            def _():
                bsum[m] = inflow[m].astype(F32) * 2.0

            @pl.when(sec > half)
            def _():
                f_copy(m, 1).wait_recv()
                bsum[m] = inflow[m].astype(F32) + skip[m].astype(F32)

        @pl.when(sec == last)
        def _():
            pull_back(m)

        def act_rows(r):
            b = bsum[m, pl.ds(r, step)]
            scale = lax.rsqrt(jnp.mean(b * b, axis=-1, keepdims=True) + 1e-06)
            x = b * scale * gain_ref[...]
            t = jnp.tanh(GELU_A * (x + GELU_B * (x * x * x)))
            y = (x * (0.5 * (1.0 + t))).astype(BF16).astype(F32)
            actf[m, pl.ds(pl.multiple_of(EDGE + r, 8), step)] = jnp.where(row_mask(r, step), y, 0.0)

        by_rows(act_rows)

        @pl.when(sec < last)
        def _():
            shifted(actf, m, False)

            @pl.when(m == 0)
            def _():
                w_copy.wait()

            def tile(n, c):
                at = pl.ds(pl.multiple_of(n * 256, 256), 256)
                total = bsum[m, :, at] + jnp.dot(
                    x5[...], w_ref[:, at], preferred_element_type=F32
                )
                fout[m, :, at] = total.astype(BF16)
                return c

            lax.fori_loop(0, chans // 256, tile, 0)
            f_copy(m, 0).start()

            @pl.when(sec < half - 1)
            def _():
                f_copy(m, 1).start()

        return carry

    lax.fori_loop(0, micro, forward, 0)

    def picker(j):
        c = lax.broadcasted_iota(jnp.int32, (chans, LANES), 0)
        lane = lax.broadcasted_iota(jnp.int32, (chans, LANES), 1)
        return jnp.where((c == j * part + lane) & (lane < part), 1.0, 0.0).astype(BF16)

    def a_copy(j):
        return remote(aslab.at[j], acol.at[q], a_send.at[j], a_recv.at[q], seq=j)

    def a_from(j):
        return remote(aslab.at[j], acol.at[j], a_send.at[j], a_recv.at[j], seq=j)

    def spread_rows():
        own = slice(EDGE + halo, EDGE + halo + rows)

        def slab(j, carry):
            pick = picker(j)
            for m in range(micro):
                aslab[j, m] = jnp.dot(
                    actf[m, own].astype(BF16), pick, preferred_element_type=F32
                ).astype(BF16)

            @pl.when(j != q)
            def _():
                a_copy(j).start()

            @pl.when(j == q)
            def _():
                acol[j] = aslab[j]

            return carry

        lax.fori_loop(0, n_seq, slab, 0)

        def take(j, carry):
            @pl.when(j != q)
            def _():
                a_from(j).wait_recv()

            at = pl.ds(pl.multiple_of(EDGE + j * rows, 8), rows)
            for m in range(micro):
                acolf[m, at] = acol[j, m].astype(F32)
            return carry

        lax.fori_loop(0, n_seq, take, 0)

        def turn(j, carry):
            for m in range(micro):
                window = acolf[m, pl.ds(pl.multiple_of(j * rows, rows), rows + 2 * EDGE)]
                for k in range(KERNEL):
                    off = EDGE + k - reach
                    a5t[j, k * LANES : (k + 1) * LANES, m * rows : (m + 1) * rows] = (
                        window[off : off + rows].T.astype(BF16)
                    )
            return carry

        lax.fori_loop(0, n_seq, turn, 0)

    @pl.when(sec < half)
    def _():
        spread_rows()

    def backward(m, carry):
        b_copy(m, 0).wait_recv()

        @pl.when(sec < half - 1)
        def _():
            b_copy(m, 1).wait_recv()
            gradf[m, EDGE : EDGE + ext] = (
                (gin[m].astype(F32) + gskip[m].astype(F32)).astype(BF16).astype(F32)
            )

        @pl.when(sec == half - 1)
        def _():
            gradf[m, EDGE : EDGE + ext] = gin[m].astype(F32) * 2.0

        @pl.when(sec >= half)
        def _():
            gradf[m, EDGE : EDGE + ext] = gin[m].astype(F32)

        gall[q, m] = gradf[m, EDGE + halo : EDGE + halo + rows].astype(BF16)
        each_way(range(4), q, m, start)
        conv_back(m)

        pull_back(m)
        return carry

    @pl.when(sec < last)
    def _():
        lax.fori_loop(0, micro, backward, 0)

    @pl.when((sec >= half) & (sec < last))
    def _():
        gather_column(lambda block: None)

    @pl.when(sec >= half)
    def _():
        gather_row(lambda block: None)

    @pl.when(sec >= half)
    def _():
        spread_rows()

    def n_copy(j):
        return remote(gslab.at[j], grecv.at[q], n_send.at[j], n_recv.at[q], seq=j)

    def n_from(j):
        return remote(gslab.at[j], grecv.at[j], n_send.at[j], n_recv.at[j], seq=j)

    gain_part = jnp.broadcast_to(jnp.sum(gain_acc[...], axis=0, keepdims=True), (16, chans))
    gain_part = gain_part.astype(BF16)

    def gain_slab(j, carry):
        gslab[j] = jnp.dot(gain_part, picker(j), preferred_element_type=F32)[0:8]

        @pl.when(j != q)
        def _():
            n_copy(j).start()

        @pl.when(j == q)
        def _():
            grecv[j] = gslab[j]

        return carry

    lax.fori_loop(0, n_seq, gain_slab, 0)

    @pl.when(sec < half)
    def _():
        gather_column(multiply)
        gather_row(multiply)

    @pl.when(sec >= half)
    def _():
        def one(j, carry):
            multiply(j)
            return carry

        lax.fori_loop(0, n_seq, one, 0)

    for k in range(KERNEL):
        out_ref[k] = acc[k * LANES : k * LANES + part].astype(BF16)

    def gain_take(j, total):
        @pl.when(j != q)
        def _():
            n_from(j).wait_recv()

        return total + grecv[j]

    gain_total = lax.fori_loop(0, n_seq, gain_take, jnp.zeros((8, LANES), F32))
    gout_ref[...] = gain_total[0:1, 0:part]

    @pl.when(sec == 0)
    def _():
        @pl.when(q < n_seq - 1)
        def _():
            e_copy(0).wait_send()

        @pl.when(q > 0)
        def _():
            e_copy(1).wait_send()

    @pl.when(sec == last)
    def _():
        @pl.when(q < n_seq - 1)
        def _():
            c_copy(0).wait_send()

        @pl.when(q > 0)
        def _():
            c_copy(1).wait_send()

    for m in range(micro):
        @pl.when(sec < last)
        def _():
            f_copy(m, 0).wait_send()

        @pl.when(sec < half - 1)
        def _():
            f_copy(m, 1).wait_send()

        @pl.when(sec > 0)
        def _():
            b_copy(m, 0).wait_send()

        @pl.when(sec > half)
        def _():
            b_copy(m, 1).wait_send()

        each_way(range(4), q, m, wait_send)
        for d in range(1, n_hi):
            @pl.when(hi - d >= 0)
            def _():
                each_way((0, 2, 3), q - d * n_lo, m, wait_send)

            @pl.when(hi + d < n_hi)
            def _():
                each_way((1, 2, 3), q + d * n_lo, m, wait_send)

        for e in range(1, n_lo):
            for h in range(n_hi):
                @pl.when(lo - e >= 0)
                def _():
                    each_way((2,), h * n_lo + lo - e, m, wait_send)

                @pl.when(lo + e < n_lo)
                def _():
                    each_way((3,), h * n_lo + lo + e, m, wait_send)

    def sent(j, carry):
        @pl.when(j != q)
        def _():
            a_copy(j).wait_send()
            n_copy(j).wait_send()

        return carry

    lax.fori_loop(0, n_seq, sent, 0)


def finish(conv_ref, gain_ref, out_ref, gout_ref):
    out_ref[0] = conv_ref[...]
    gout_ref[...] = gain_ref[...]


def shards(sections, n_seq, base_ids, stem_weight, conv_weight, block_gain, cotangent):
    micro, rows, chans = cotangent.shape
    n_lo = max(1, n_seq // 4)
    halo = -(-4 * (sections - 1) // 16) * 16
    ext = rows + 2 * halo
    e_halo = halo + 16
    part = chans // n_seq
    vmem, dma = pltpu.VMEM, pltpu.SemaphoreType.DMA
    flow = vmem((micro, ext, chans), BF16)
    scratch = [
        vmem((KERNEL * chans, chans), BF16),
        vmem((LANES, chans), F32),
        vmem((micro, rows + 2 * e_halo, LANES), F32),
        vmem((micro, ext, chans), F32),
        vmem((micro, ext + 2 * EDGE, chans), F32),
        vmem((ext, KERNEL * chans), BF16),
        vmem((micro, ext + 2 * EDGE, chans), F32),
        vmem((micro, ext, chans), F32),
        flow, flow, flow, flow, flow, flow,
        vmem((2, micro, halo, chans), BF16),
        vmem((n_seq, micro, rows, LANES), BF16),
        vmem((n_seq, micro, rows, LANES), BF16),
        vmem((micro, n_seq * rows + 2 * EDGE, LANES), F32),
        vmem((n_seq, KERNEL * LANES, micro * rows), BF16),
        vmem((n_seq, micro, rows, chans), BF16),
        vmem((KERNEL * LANES, chans), F32),
        vmem((8, chans), F32),
        vmem((n_seq, 8, LANES), F32),
        vmem((n_seq, 8, LANES), F32),
        dma((2,)), dma((2,)), dma((2,)), dma((2,)),
        dma((micro, 2)), dma((micro, 2)), dma((micro, 2)), dma((micro, 2)),
        dma((n_seq,)), dma((n_seq,)), dma((n_seq,)), dma((n_seq,)),
        dma((n_seq, micro, 4)), dma((n_seq, micro)), dma,
    ]
    conv_grad, gain_grad = pl.pallas_call(
        functools.partial(level_kernel, sections, n_seq, n_lo, micro, rows, chans, halo),
        out_shape=(
            jax.ShapeDtypeStruct((KERNEL, part, chans), BF16),
            jax.ShapeDtypeStruct((1, part), F32),
        ),
        in_specs=[pl.BlockSpec(memory_space=pl.ANY if i == 2 else vmem) for i in range(5)],
        out_specs=(pl.BlockSpec(memory_space=pltpu.VMEM),) * 2,
        scratch_shapes=scratch,
        compiler_params=pltpu.CompilerParams(
            collective_id=0, has_side_effects=True, vmem_limit_bytes=58 * 2**20
        ),
    )(base_ids, stem_weight, conv_weight[0].reshape(KERNEL * chans, chans), block_gain, cotangent)
    whole = pl.BlockSpec(memory_space=vmem)
    conv_grad, gain_grad = pl.pallas_call(
        finish,
        out_shape=(
            jax.ShapeDtypeStruct((1, KERNEL, part, chans), BF16),
            jax.ShapeDtypeStruct((1, part), F32),
        ),
        in_specs=[whole, whole],
        out_specs=(whole, whole),
    )(conv_grad, gain_grad)
    return conv_grad, gain_grad


def solution(mesh):
    placed = (
        P(None, "seq"),
        P(),
        P("section", None, None, None),
        P("section", None),
        P(None, "seq", None),
    )
    return jax.shard_map(
        functools.partial(shards, mesh.shape["section"], mesh.shape["seq"]),
        mesh=mesh,
        in_specs=placed,
        out_specs=(P("section", None, "seq", None), P("section", "seq")),
        check_vma=False,
    )
```

```python
import functools

import jax
import jax.numpy as jnp
from jax import lax
from jax.experimental import pallas as pl
from jax.experimental.pallas import tpu as pltpu
from jax.sharding import PartitionSpec as P

KERNEL = 5
STEM_K = 15
BASES = 4
LANES = 128
EDGE = 8
F32, BF16 = jnp.float32, jnp.bfloat16
FULL, MAIN, SIDE = 0, 1, 2
GELU_A, GELU_B = 0.7978845608028654, 0.044715


def remote(src, dst, send_sem, recv_sem, **where):
    return pltpu.make_async_remote_copy(
        src_ref=src,
        dst_ref=dst,
        send_sem=send_sem,
        recv_sem=recv_sem,
        device_id=where,
        device_id_type=pl.DeviceIdType.MESH,
    )


def level_kernel(
    sections, n_seq, n_lo, micro, rows, chans, halo,
    ids_ref, stem_ref, w_hbm, gain_ref, cot_ref,
    out_ref, gout_ref,
    w_ref, stemf, ebuf, bsum, actf, x5, gradf, gact, inflow, skip, fout, gin, gskip, gsend, coth,
    aslab, acol, acolf, a5t, gall, acc, gain_acc, gslab, grecv,
    e_send, e_recv, c_send, c_recv, f_send, f_recv, b_send, b_recv,
    a_send, a_recv, n_send, n_recv, ag_send, ag_recv, w_sem,
    rbuf, r_send, r_recv, u_send, u_recv, d_send, d_recv,
):
    sec, q = lax.axis_index("section"), lax.axis_index("seq")
    n_hi = n_seq // n_lo
    hi, lo = q // n_lo, q % n_lo
    half = sections // 2
    ext = rows + 2 * halo
    e_halo = halo + 16
    part = chans // n_seq
    reach = (KERNEL - 1) // 2
    cut = chans * 2 // 3 // LANES * LANES
    last = sections - 1
    mirror_sec = last - sec
    step = 32
    tokens = rows * n_seq

    w_copy = pltpu.make_async_copy(w_hbm, w_ref, w_sem)
    w_copy.start()
    barrier = pltpu.get_barrier_semaphore()
    for d in range(1, n_seq):
        pl.semaphore_signal(
            barrier, inc=1, device_id={"seq": (q + d) % n_seq}, device_id_type=pl.DeviceIdType.MESH
        )
    for d in range(1, sections):
        pl.semaphore_signal(
            barrier, inc=1, device_id={"section": (sec + d) % sections},
            device_id_type=pl.DeviceIdType.MESH,
        )
    pl.semaphore_wait(barrier, n_seq + sections - 2)

    def e_copy(side):
        if side == 0:
            src, dst, to = ebuf.at[:, rows : e_halo + rows], ebuf.at[:, 0:e_halo], q + 1
        else:
            src, dst, to = ebuf.at[:, e_halo : 2 * e_halo], ebuf.at[:, e_halo + rows :], q - 1
        return remote(src, dst, e_send.at[side], e_recv.at[side], seq=to)

    def c_copy(side):
        if side == 0:
            src, dst, to = cot_ref.at[:, rows - halo : rows], coth.at[0], q + 1
        else:
            src, dst, to = cot_ref.at[:, 0:halo], coth.at[1], q - 1
        return remote(src, dst, c_send.at[side], c_recv.at[side], seq=to)

    def gather_copy(kind, block, m, way):
        to = [q + n_lo, q - n_lo, q + 1, q - 1][way]
        if kind == SIDE:
            here, sends, lands = rbuf.at[block, m], r_send, r_recv
        else:
            here = gall.at[block, m] if kind == FULL else gall.at[block, m, :, 0:cut]
            sends, lands = ag_send, ag_recv
        return remote(here, here, sends.at[block, m, way], lands.at[block, m], seq=to)

    def raise_copy(m):
        return remote(
            gall.at[q, m, :, cut:], rbuf.at[q, m], u_send.at[m], u_recv.at[m], section=sec + half
        )

    def lower_copy(block, m, to):
        return remote(
            rbuf.at[block, m], gall.at[block, m, :, cut:], d_send.at[block, m],
            d_recv.at[block, m], section=to,
        )

    up, down, right, left = hi < n_hi - 1, hi > 0, lo < n_lo - 1, lo > 0

    def each_way(kind, ways, block, m, act):
        for way in ways:
            @pl.when([up, down, right, left][way])
            def _():
                act(gather_copy(kind, block, m, way))

    def start(copy):
        copy.start()

    def wait_send(copy):
        copy.wait_send()

    for ref in (actf, gradf):
        ref[:, 0:EDGE] = jnp.zeros((micro, EDGE, chans), F32)
        ref[:, EDGE + ext :] = jnp.zeros((micro, EDGE, chans), F32)
    acolf[:, 0:EDGE] = jnp.zeros((micro, EDGE, LANES), F32)
    acolf[:, EDGE + tokens :] = jnp.zeros((micro, EDGE, LANES), F32)
    gain_acc[...] = jnp.zeros_like(gain_acc)
    acc[...] = jnp.zeros_like(acc)

    @pl.when(sec == 0)
    def _():
        lane = lax.broadcasted_iota(jnp.int32, (rows, LANES), 1)
        wanted = jnp.where(lane < STEM_K * BASES, lane % BASES, -1).astype(F32)
        for m in range(micro):
            ids = jnp.broadcast_to(ids_ref[m : m + 1, :].astype(F32), (LANES, rows)).T
            ebuf[m, e_halo : e_halo + rows] = jnp.where(ids == wanted, 1.0, 0.0)

        @pl.when(q < n_seq - 1)
        def _():
            e_copy(0).start()

        @pl.when(q > 0)
        def _():
            e_copy(1).start()

        stemf[...] = jnp.zeros_like(stemf)
        for k in range(STEM_K):
            stemf[k * BASES : (k + 1) * BASES] = stem_ref[k].astype(F32)

        @pl.when(q == 0)
        def _():
            ebuf[:, 0:e_halo] = jnp.zeros((micro, e_halo, LANES), F32)

        @pl.when(q == n_seq - 1)
        def _():
            ebuf[:, e_halo + rows :] = jnp.zeros((micro, e_halo, LANES), F32)

        @pl.when(q > 0)
        def _():
            e_copy(0).wait_recv()

        @pl.when(q < n_seq - 1)
        def _():
            e_copy(1).wait_recv()

    def row_mask(first, count):
        place = lax.broadcasted_iota(jnp.int32, (count, 1), 0) + (first + q * rows - halo)
        return (place >= 0) & (place < tokens)

    def shifted(ref, m, flip):
        for k in range(KERNEL):
            off = EDGE + (reach - k if flip else k - reach)
            x5[:, k * chans : (k + 1) * chans] = ref[m, off : off + ext].astype(BF16)

    def conv_back(m):
        shifted(gradf, m, True)

        def tile(n, carry):
            at = pl.ds(pl.multiple_of(n * 256, 256), 256)
            total = jnp.zeros((ext, 256), F32)
            for k in range(KERNEL):
                total = total + lax.dot_general(
                    x5[:, k * chans : (k + 1) * chans],
                    w_ref[pl.ds(pl.multiple_of(k * chans + n * 256, 256), 256), :],
                    (((1,), (1,)), ((), ())),
                    preferred_element_type=F32,
                )
            gact[m, :, at] = total
            return carry

        lax.fori_loop(0, chans // 256, tile, 0)

    def multiply(block):
        def tile(n, c):
            at = pl.ds(pl.multiple_of(n * 256, 256), 256)
            acc[:, at] += jnp.dot(
                a5t[block], gall[block, :, :, at].reshape(micro * rows, 256),
                preferred_element_type=F32,
            )
            return c

        lax.fori_loop(0, chans // 256, tile, 0)

    def column_blocks(body):
        for d in range(1, n_hi):
            @pl.when(hi - d >= 0)
            def _():
                body(q - d * n_lo, 0, (0, 2, 3))

            @pl.when(hi + d < n_hi)
            def _():
                body(q + d * n_lo, 1, (1, 2, 3))

    def row_blocks(body):
        for e in range(1, n_lo):
            for d in range(n_hi):
                for side in (-1, 1) if d else (1,):
                    h = hi + side * d

                    @pl.when((h >= 0) & (h < n_hi) & (lo - e >= 0))
                    def _():
                        body(h * n_lo + lo - e, 2, (2,))

                    @pl.when((h >= 0) & (h < n_hi) & (lo + e < n_lo))
                    def _():
                        body(h * n_lo + lo + e, 3, (3,))

    def taking(kind, then=None):
        def body(block, way, onward):
            for m in range(micro):
                gather_copy(kind, block, m, way).wait_recv()
                each_way(kind, onward, block, m, start)
                if kind == SIDE:
                    lower_copy(block, m, sec - half).start()
            if then is not None:
                then(block)

        return body

    def joined(block, way=0, onward=()):
        for m in range(micro):
            lower_copy(block, m, sec + half).wait_recv()
        multiply(block)

    def relay():
        for m in range(micro):
            raise_copy(m).wait_recv()
            each_way(SIDE, range(4), q, m, start)
        column_blocks(taking(SIDE))
        row_blocks(taking(SIDE))

    def drained(kind):
        def body(block, way, onward):
            for m in range(micro):
                each_way(kind, onward, block, m, wait_send)
                if kind == SIDE:
                    lower_copy(block, m, sec - half).wait_send()

        for m in range(micro):
            each_way(kind, range(4), q, m, wait_send)
        column_blocks(body)
        row_blocks(body)

    @pl.when(sec == last)
    def _():
        @pl.when(q < n_seq - 1)
        def _():
            c_copy(0).start()

        @pl.when(q > 0)
        def _():
            c_copy(1).start()

        gall[q] = cot_ref[...]
        for m in range(micro):
            each_way(FULL, range(4), q, m, start)
        gradf[:, EDGE + halo : EDGE + halo + rows] = cot_ref[...].astype(F32)

        @pl.when(q == 0)
        def _():
            gradf[:, EDGE : EDGE + halo] = jnp.zeros((micro, halo, chans), F32)

        @pl.when(q == n_seq - 1)
        def _():
            gradf[:, EDGE + halo + rows : EDGE + ext] = jnp.zeros((micro, halo, chans), F32)

        @pl.when(q > 0)
        def _():
            c_copy(0).wait_recv()
            gradf[:, EDGE : EDGE + halo] = coth[0].astype(F32)

        @pl.when(q < n_seq - 1)
        def _():
            c_copy(1).wait_recv()
            gradf[:, EDGE + halo + rows : EDGE + ext] = coth[1].astype(F32)

        w_copy.wait()

        def each(m, carry):
            conv_back(m)
            return carry

        lax.fori_loop(0, micro, each, 0)
        column_blocks(taking(FULL))

    def f_copy(m, kind):
        to = sec + 1 if kind == 0 else mirror_sec
        dst = inflow if kind == 0 else skip
        return remote(fout.at[m], dst.at[m], f_send.at[m, kind], f_recv.at[m, kind], section=to)

    def b_copy(m, kind):
        to = sec - 1 if kind == 0 else mirror_sec
        dst = gin if kind == 0 else gskip
        return remote(gsend.at[m], dst.at[m], b_send.at[m, kind], b_recv.at[m, kind], section=to)

    def by_rows(body):
        def one(i, carry):
            body(pl.multiple_of(i * step, step))
            return carry

        lax.fori_loop(0, ext // step, one, 0, unroll=True)

    def pull_back(m):
        def pull_rows(r):
            at = pl.ds(r, step)
            b, grad = bsum[m, at], gact[m, at]
            scale = lax.rsqrt(jnp.mean(b * b, axis=-1, keepdims=True) + 1e-06)
            unit = b * scale
            x = unit * gain_ref[...]
            t = jnp.tanh(GELU_A * (x + GELU_B * (x * x * x)))
            slope = 0.5 * (1.0 + t) + (0.5 * GELU_A) * x * (1.0 - t * t) * (
                1.0 + (3.0 * GELU_B) * (x * x)
            )
            d_pre = grad * slope
            d_unit = d_pre * gain_ref[...]
            place = lax.broadcasted_iota(jnp.int32, (step, 1), 0) + r
            mine = (place >= halo) & (place < halo + rows)
            terms = jnp.where(mine, d_pre * unit, 0.0)
            gain_acc[...] += jnp.sum(terms.reshape(step // 8, 8, chans), axis=0)
            pulled = scale * (d_unit - unit * jnp.mean(d_unit * unit, axis=-1, keepdims=True))
            whole = gradf[m, pl.ds(pl.multiple_of(EDGE + r, 8), step)] + pulled
            gsend[m, at] = jnp.where(row_mask(r, step), whole, 0.0).astype(BF16)

        by_rows(pull_rows)

        @pl.when(sec > 0)
        def _():
            b_copy(m, 0).start()

            @pl.when(sec > half)
            def _():
                b_copy(m, 1).start()


    def forward(m, carry):
        @pl.when(sec == 0)
        def _():
            tap = lax.broadcasted_iota(jnp.int32, (ext, LANES), 1) // BASES
            hot = jnp.zeros((ext, LANES), F32)
            for k in range(STEM_K):
                off = e_halo - halo + k - (STEM_K - 1) // 2
                hot = jnp.where(tap == k, ebuf[m, off : off + ext], hot)
            stem = jnp.dot(
                hot.astype(BF16), stemf[...].astype(BF16), preferred_element_type=F32
            )
            bsum[m] = stem.astype(BF16).astype(F32)

        @pl.when(sec > 0)
        def _():
            f_copy(m, 0).wait_recv()

            @pl.when(sec < half)
            def _():
                bsum[m] = inflow[m].astype(F32)

            @pl.when(sec == half)
            def _():
                bsum[m] = inflow[m].astype(F32) * 2.0

            @pl.when(sec > half)
            def _():
                f_copy(m, 1).wait_recv()
                bsum[m] = inflow[m].astype(F32) + skip[m].astype(F32)

        @pl.when(sec == last)
        def _():
            pull_back(m)

        def act_rows(r):
            b = bsum[m, pl.ds(r, step)]
            scale = lax.rsqrt(jnp.mean(b * b, axis=-1, keepdims=True) + 1e-06)
            x = b * scale * gain_ref[...]
            t = jnp.tanh(GELU_A * (x + GELU_B * (x * x * x)))
            y = (x * (0.5 * (1.0 + t))).astype(BF16).astype(F32)
            actf[m, pl.ds(pl.multiple_of(EDGE + r, 8), step)] = jnp.where(row_mask(r, step), y, 0.0)

        by_rows(act_rows)

        @pl.when(sec < last)
        def _():
            shifted(actf, m, False)

            @pl.when(m == 0)
            def _():
                w_copy.wait()

            def tile(n, c):
                at = pl.ds(pl.multiple_of(n * 256, 256), 256)
                total = bsum[m, :, at] + jnp.dot(
                    x5[...], w_ref[:, at], preferred_element_type=F32
                )
                fout[m, :, at] = total.astype(BF16)
                return c

            lax.fori_loop(0, chans // 256, tile, 0)
            f_copy(m, 0).start()

            @pl.when(sec < half - 1)
            def _():
                f_copy(m, 1).start()

        return carry

    lax.fori_loop(0, micro, forward, 0)

    def picker(j):
        c = lax.broadcasted_iota(jnp.int32, (chans, LANES), 0)
        lane = lax.broadcasted_iota(jnp.int32, (chans, LANES), 1)
        return jnp.where((c == j * part + lane) & (lane < part), 1.0, 0.0).astype(BF16)

    def a_copy(j):
        return remote(aslab.at[j], acol.at[q], a_send.at[j], a_recv.at[q], seq=j)

    def a_from(j):
        return remote(aslab.at[j], acol.at[j], a_send.at[j], a_recv.at[j], seq=j)

    def spread_rows():
        own = slice(EDGE + halo, EDGE + halo + rows)

        def slab(j, carry):
            pick = picker(j)
            for m in range(micro):
                aslab[j, m] = jnp.dot(
                    actf[m, own].astype(BF16), pick, preferred_element_type=F32
                ).astype(BF16)

            @pl.when(j != q)
            def _():
                a_copy(j).start()

            @pl.when(j == q)
            def _():
                acol[j] = aslab[j]

            return carry

        lax.fori_loop(0, n_seq, slab, 0)

        def take(j, carry):
            @pl.when(j != q)
            def _():
                a_from(j).wait_recv()

            at = pl.ds(pl.multiple_of(EDGE + j * rows, 8), rows)
            for m in range(micro):
                acolf[m, at] = acol[j, m].astype(F32)
            return carry

        lax.fori_loop(0, n_seq, take, 0)

        eye = jnp.where(
            lax.broadcasted_iota(jnp.int32, (LANES, LANES), 0)
            == lax.broadcasted_iota(jnp.int32, (LANES, LANES), 1), 1.0, 0.0,
        ).astype(BF16)

        def turn(j, carry):
            for m in range(micro):
                window = acolf[m, pl.ds(pl.multiple_of(j * rows, rows), rows + 2 * EDGE)]
                for k in range(KERNEL):
                    off = EDGE + k - reach
                    a5t[j, k * LANES : (k + 1) * LANES, m * rows : (m + 1) * rows] = (
                        lax.dot_general(
                            eye, window[off : off + rows].astype(BF16),
                            (((1,), (1,)), ((), ())), preferred_element_type=F32,
                        ).astype(BF16)
                    )
            return carry

        lax.fori_loop(0, n_seq, turn, 0)

    @pl.when(sec < half)
    def _():
        spread_rows()

    def backward(m, carry):
        b_copy(m, 0).wait_recv()

        @pl.when(sec < half - 1)
        def _():
            b_copy(m, 1).wait_recv()
            gradf[m, EDGE : EDGE + ext] = (
                (gin[m].astype(F32) + gskip[m].astype(F32)).astype(BF16).astype(F32)
            )

        @pl.when(sec == half - 1)
        def _():
            gradf[m, EDGE : EDGE + ext] = gin[m].astype(F32) * 2.0

        @pl.when(sec >= half)
        def _():
            gradf[m, EDGE : EDGE + ext] = gin[m].astype(F32)

        gall[q, m] = gradf[m, EDGE + halo : EDGE + halo + rows].astype(BF16)

        @pl.when(sec < half)
        def _():
            each_way(MAIN, range(4), q, m, start)
            raise_copy(m).start()

        @pl.when(sec >= half)
        def _():
            each_way(FULL, range(4), q, m, start)

        conv_back(m)
        pull_back(m)
        return carry

    @pl.when(sec < last)
    def _():
        lax.fori_loop(0, micro, backward, 0)

    @pl.when(sec >= half)
    def _():
        spread_rows()

        @pl.when(sec < last)
        def _():
            column_blocks(taking(FULL, multiply))

        relay()

    def n_copy(j):
        return remote(gslab.at[j], grecv.at[q], n_send.at[j], n_recv.at[q], seq=j)

    def n_from(j):
        return remote(gslab.at[j], grecv.at[j], n_send.at[j], n_recv.at[j], seq=j)

    gain_part = jnp.broadcast_to(jnp.sum(gain_acc[...], axis=0, keepdims=True), (16, chans))
    gain_part = gain_part.astype(BF16)

    def gain_slab(j, carry):
        gslab[j] = jnp.dot(gain_part, picker(j), preferred_element_type=F32)[0:8]

        @pl.when(j != q)
        def _():
            n_copy(j).start()

        @pl.when(j == q)
        def _():
            grecv[j] = gslab[j]

        return carry

    lax.fori_loop(0, n_seq, gain_slab, 0)

    multiply(q)

    @pl.when(sec < half)
    def _():
        column_blocks(taking(MAIN))
        column_blocks(joined)
        row_blocks(taking(MAIN, joined))

    @pl.when(sec >= half)
    def _():
        @pl.when(sec == last)
        def _():
            column_blocks(lambda block, way, onward: multiply(block))

        row_blocks(taking(FULL, multiply))

    for k in range(KERNEL):
        out_ref[k] = acc[k * LANES : k * LANES + part].astype(BF16)

    def gain_take(j, total):
        @pl.when(j != q)
        def _():
            n_from(j).wait_recv()

        return total + grecv[j]

    gain_total = lax.fori_loop(0, n_seq, gain_take, jnp.zeros((8, LANES), F32))
    gout_ref[...] = gain_total[0:1, 0:part]

    @pl.when(sec == 0)
    def _():
        @pl.when(q < n_seq - 1)
        def _():
            e_copy(0).wait_send()

        @pl.when(q > 0)
        def _():
            e_copy(1).wait_send()

    @pl.when(sec == last)
    def _():
        @pl.when(q < n_seq - 1)
        def _():
            c_copy(0).wait_send()

        @pl.when(q > 0)
        def _():
            c_copy(1).wait_send()

    for m in range(micro):
        @pl.when(sec < last)
        def _():
            f_copy(m, 0).wait_send()

        @pl.when(sec < half - 1)
        def _():
            f_copy(m, 1).wait_send()

        @pl.when(sec > 0)
        def _():
            b_copy(m, 0).wait_send()

        @pl.when(sec > half)
        def _():
            b_copy(m, 1).wait_send()

        @pl.when(sec < half)
        def _():
            raise_copy(m).wait_send()

    @pl.when(sec < half)
    def _():
        drained(MAIN)

    @pl.when(sec >= half)
    def _():
        drained(FULL)
        drained(SIDE)

    def sent(j, carry):
        @pl.when(j != q)
        def _():
            a_copy(j).wait_send()
            n_copy(j).wait_send()

        return carry

    lax.fori_loop(0, n_seq, sent, 0)


def finish(conv_ref, gain_ref, out_ref, gout_ref):
    out_ref[0] = conv_ref[...]
    gout_ref[...] = gain_ref[...]


def shards(sections, n_seq, base_ids, stem_weight, conv_weight, block_gain, cotangent):
    micro, rows, chans = cotangent.shape
    n_lo = max(1, n_seq // 4)
    halo = -(-4 * (sections - 1) // 16) * 16
    ext = rows + 2 * halo
    e_halo = halo + 16
    part = chans // n_seq
    vmem, dma = pltpu.VMEM, pltpu.SemaphoreType.DMA
    flow = vmem((micro, ext, chans), BF16)
    scratch = [
        vmem((KERNEL * chans, chans), BF16),
        vmem((LANES, chans), F32),
        vmem((micro, rows + 2 * e_halo, LANES), F32),
        vmem((micro, ext, chans), F32),
        vmem((micro, ext + 2 * EDGE, chans), F32),
        vmem((ext, KERNEL * chans), BF16),
        vmem((micro, ext + 2 * EDGE, chans), F32),
        vmem((micro, ext, chans), F32),
        flow, flow, flow, flow, flow, flow,
        vmem((2, micro, halo, chans), BF16),
        vmem((n_seq, micro, rows, LANES), BF16),
        vmem((n_seq, micro, rows, LANES), BF16),
        vmem((micro, n_seq * rows + 2 * EDGE, LANES), F32),
        vmem((n_seq, KERNEL * LANES, micro * rows), BF16),
        vmem((n_seq, micro, rows, chans), BF16),
        vmem((KERNEL * LANES, chans), F32),
        vmem((8, chans), F32),
        vmem((n_seq, 8, LANES), F32),
        vmem((n_seq, 8, LANES), F32),
        dma((2,)), dma((2,)), dma((2,)), dma((2,)),
        dma((micro, 2)), dma((micro, 2)), dma((micro, 2)), dma((micro, 2)),
        dma((n_seq,)), dma((n_seq,)), dma((n_seq,)), dma((n_seq,)),
        dma((n_seq, micro, 4)), dma((n_seq, micro)), dma,
        vmem((n_seq, micro, rows, chans - chans * 2 // 3 // LANES * LANES), BF16),
        dma((n_seq, micro, 4)), dma((n_seq, micro)), dma((micro,)), dma((micro,)),
        dma((n_seq, micro)), dma((n_seq, micro)),
    ]
    conv_grad, gain_grad = pl.pallas_call(
        functools.partial(level_kernel, sections, n_seq, n_lo, micro, rows, chans, halo),
        out_shape=(
            jax.ShapeDtypeStruct((KERNEL, part, chans), BF16),
            jax.ShapeDtypeStruct((1, part), F32),
        ),
        in_specs=[pl.BlockSpec(memory_space=pl.ANY if i == 2 else vmem) for i in range(5)],
        out_specs=(pl.BlockSpec(memory_space=pltpu.VMEM),) * 2,
        scratch_shapes=scratch,
        compiler_params=pltpu.CompilerParams(
            collective_id=0, has_side_effects=True, vmem_limit_bytes=58 * 2**20
        ),
    )(base_ids, stem_weight, conv_weight[0].reshape(KERNEL * chans, chans), block_gain, cotangent)
    whole = pl.BlockSpec(memory_space=vmem)
    conv_grad, gain_grad = pl.pallas_call(
        finish,
        out_shape=(
            jax.ShapeDtypeStruct((1, KERNEL, part, chans), BF16),
            jax.ShapeDtypeStruct((1, part), F32),
        ),
        in_specs=[whole, whole],
        out_specs=(whole, whole),
    )(conv_grad, gain_grad)
    return conv_grad, gain_grad


def solution(mesh):
    placed = (
        P(None, "seq"),
        P(),
        P("section", None, None, None),
        P("section", None),
        P(None, "seq", None),
    )
    return jax.shard_map(
        functools.partial(shards, mesh.shape["section"], mesh.shape["seq"]),
        mesh=mesh,
        in_specs=placed,
        out_specs=(P("section", None, "seq", None), P("section", "seq")),
        check_vma=False,
    )
```

```python
import functools

import jax
import jax.numpy as jnp
from jax import lax
from jax.experimental import pallas as pl
from jax.experimental.pallas import tpu as pltpu
from jax.sharding import PartitionSpec as P

KERNEL = 5
STEM_K = 15
BASES = 4
LANES = 128
EDGE = 8
F32, BF16 = jnp.float32, jnp.bfloat16
FULL, MAIN, SIDE, FIRST = 0, 1, 2, 3
GELU_A, GELU_B = 0.7978845608028654, 0.044715


def remote(src, dst, send_sem, recv_sem, **where):
    return pltpu.make_async_remote_copy(
        src_ref=src,
        dst_ref=dst,
        send_sem=send_sem,
        recv_sem=recv_sem,
        device_id=where,
        device_id_type=pl.DeviceIdType.MESH,
    )


def level_kernel(
    sections, n_seq, n_lo, micro, rows, chans, halo,
    ids_ref, stem_ref, w_hbm, gain_ref, cot_ref,
    out_ref, gout_ref,
    w_ref, stemf, ebuf, bsum, actf, x5, gradf, gact, inflow, skip, fout, gin, gskip, gsend, coth,
    aslab, acol, acolf, a5t, gall, acc, gain_acc, gslab, grecv,
    e_send, e_recv, c_send, c_recv, f_send, f_recv, b_send, b_recv,
    a_send, a_recv, n_send, n_recv, ag_send, ag_recv, w_sem,
    rbuf, r_send, r_recv, u_send, u_recv, d_send, d_recv,
):
    sec, q = lax.axis_index("section"), lax.axis_index("seq")
    n_hi = n_seq // n_lo
    hi, lo = q // n_lo, q % n_lo
    half = sections // 2
    ext = rows + 2 * halo
    e_halo = halo + 16
    part = chans // n_seq
    reach = (KERNEL - 1) // 2
    cut = chans * 2 // 3 // LANES * LANES
    last = sections - 1
    mirror_sec = last - sec
    step = 32
    tokens = rows * n_seq

    w_copy = pltpu.make_async_copy(w_hbm, w_ref, w_sem)
    w_copy.start()
    barrier = pltpu.get_barrier_semaphore()
    for d in range(1, n_seq):
        pl.semaphore_signal(
            barrier, inc=1, device_id={"seq": (q + d) % n_seq}, device_id_type=pl.DeviceIdType.MESH
        )
    for d in range(1, sections):
        pl.semaphore_signal(
            barrier, inc=1, device_id={"section": (sec + d) % sections},
            device_id_type=pl.DeviceIdType.MESH,
        )
    pl.semaphore_wait(barrier, n_seq + sections - 2)

    def e_copy(side):
        if side == 0:
            src, dst, to = ebuf.at[:, rows : e_halo + rows], ebuf.at[:, 0:e_halo], q + 1
        else:
            src, dst, to = ebuf.at[:, e_halo : 2 * e_halo], ebuf.at[:, e_halo + rows :], q - 1
        return remote(src, dst, e_send.at[side], e_recv.at[side], seq=to)

    def c_copy(side):
        if side == 0:
            src, dst, to = cot_ref.at[:, rows - halo : rows], coth.at[0], q + 1
        else:
            src, dst, to = cot_ref.at[:, 0:halo], coth.at[1], q - 1
        return remote(src, dst, c_send.at[side], c_recv.at[side], seq=to)

    def gather_copy(kind, block, m, way):
        to = [q + n_lo, q - n_lo, q + 1, q - 1][way]
        if kind >= SIDE:
            slot = kind - SIDE
            here, sends, lands = rbuf.at[slot, block, m], r_send.at[slot], r_recv.at[slot]
        else:
            here = gall.at[block, m] if kind == FULL else gall.at[block, m, :, 0:cut]
            sends, lands = ag_send, ag_recv
        return remote(here, here, sends.at[block, m, way], lands.at[block, m], seq=to)

    def raise_copy(kind, m):
        slot = kind - SIDE
        return remote(
            gall.at[q, m, :, cut:], rbuf.at[slot, q, m], u_send.at[m], u_recv.at[slot, m],
            section=last if kind == FIRST else sec + half,
        )

    def lower_copy(kind, block, m):
        slot = kind - SIDE
        return remote(
            rbuf.at[slot, block, m], gall.at[block, m, :, cut:], d_send.at[slot, block, m],
            d_recv.at[block, m], section=0 if kind == FIRST else sec - half,
        )

    up, down, right, left = hi < n_hi - 1, hi > 0, lo < n_lo - 1, lo > 0

    def each_way(kind, ways, block, m, act):
        for way in ways:
            @pl.when([up, down, right, left][way])
            def _():
                act(gather_copy(kind, block, m, way))

    def start(copy):
        copy.start()

    def wait_send(copy):
        copy.wait_send()

    for ref in (actf, gradf):
        ref[:, 0:EDGE] = jnp.zeros((micro, EDGE, chans), F32)
        ref[:, EDGE + ext :] = jnp.zeros((micro, EDGE, chans), F32)
    acolf[:, 0:EDGE] = jnp.zeros((micro, EDGE, LANES), F32)
    acolf[:, EDGE + tokens :] = jnp.zeros((micro, EDGE, LANES), F32)
    gain_acc[...] = jnp.zeros_like(gain_acc)
    acc[...] = jnp.zeros_like(acc)

    @pl.when(sec == 0)
    def _():
        lane = lax.broadcasted_iota(jnp.int32, (rows, LANES), 1)
        wanted = jnp.where(lane < STEM_K * BASES, lane % BASES, -1).astype(F32)
        for m in range(micro):
            ids = jnp.broadcast_to(ids_ref[m : m + 1, :].astype(F32), (LANES, rows)).T
            ebuf[m, e_halo : e_halo + rows] = jnp.where(ids == wanted, 1.0, 0.0)

        @pl.when(q < n_seq - 1)
        def _():
            e_copy(0).start()

        @pl.when(q > 0)
        def _():
            e_copy(1).start()

        stemf[...] = jnp.zeros_like(stemf)
        for k in range(STEM_K):
            stemf[k * BASES : (k + 1) * BASES] = stem_ref[k].astype(F32)

        @pl.when(q == 0)
        def _():
            ebuf[:, 0:e_halo] = jnp.zeros((micro, e_halo, LANES), F32)

        @pl.when(q == n_seq - 1)
        def _():
            ebuf[:, e_halo + rows :] = jnp.zeros((micro, e_halo, LANES), F32)

        @pl.when(q > 0)
        def _():
            e_copy(0).wait_recv()

        @pl.when(q < n_seq - 1)
        def _():
            e_copy(1).wait_recv()

    def row_mask(first, count):
        place = lax.broadcasted_iota(jnp.int32, (count, 1), 0) + (first + q * rows - halo)
        return (place >= 0) & (place < tokens)

    def shifted(ref, m, flip):
        for k in range(KERNEL):
            off = EDGE + (reach - k if flip else k - reach)
            x5[:, k * chans : (k + 1) * chans] = ref[m, off : off + ext].astype(BF16)

    def conv_back(m):
        shifted(gradf, m, True)

        def tile(n, carry):
            at = pl.ds(pl.multiple_of(n * 256, 256), 256)
            total = jnp.zeros((ext, 256), F32)
            for k in range(KERNEL):
                total = total + lax.dot_general(
                    x5[:, k * chans : (k + 1) * chans],
                    w_ref[pl.ds(pl.multiple_of(k * chans + n * 256, 256), 256), :],
                    (((1,), (1,)), ((), ())),
                    preferred_element_type=F32,
                )
            gact[m, :, at] = total
            return carry

        lax.fori_loop(0, chans // 256, tile, 0)

    def multiply(block):
        def tile(n, c):
            at = pl.ds(pl.multiple_of(n * 256, 256), 256)
            acc[:, at] += jnp.dot(
                a5t[block], gall[block, :, :, at].reshape(micro * rows, 256),
                preferred_element_type=F32,
            )
            return c

        lax.fori_loop(0, chans // 256, tile, 0)

    def column_blocks(body, distances=range(1, n_hi)):
        for d in distances:
            @pl.when(hi - d >= 0)
            def _():
                body(q - d * n_lo, 0, (0, 2, 3))

            @pl.when(hi + d < n_hi)
            def _():
                body(q + d * n_lo, 1, (1, 2, 3))

    def row_blocks(body):
        for e in range(1, n_lo):
            for d in range(n_hi):
                for side in (-1, 1) if d else (1,):
                    h = hi + side * d

                    @pl.when((h >= 0) & (h < n_hi) & (lo - e >= 0))
                    def _():
                        body(h * n_lo + lo - e, 2, (2,))

                    @pl.when((h >= 0) & (h < n_hi) & (lo + e < n_lo))
                    def _():
                        body(h * n_lo + lo + e, 3, (3,))

    def taking(kind, then=None):
        def body(block, way, onward):
            for m in range(micro):
                gather_copy(kind, block, m, way).wait_recv()
                each_way(kind, onward, block, m, start)
                if kind >= SIDE:
                    lower_copy(kind, block, m).start()
            if then is not None:
                then(block)

        return body

    def joined(block, way=0, onward=()):
        for m in range(micro):
            remote(
                rbuf.at[0, block, m], gall.at[block, m, :, cut:], d_send.at[0, block, m],
                d_recv.at[block, m], section=last,
            ).wait_recv()
        multiply(block)

    def relay(kinds):
        def stage(kind, at):
            if at == 0:
                for m in range(micro):
                    raise_copy(kind, m).wait_recv()
                    each_way(kind, range(4), q, m, start)
            elif at < n_hi:
                column_blocks(taking(kind), (at,))
            elif at == n_hi:
                row_blocks(taking(kind))

        for at in range(n_hi + len(kinds)):
            for lag, kind in enumerate(kinds):
                if at >= lag:
                    stage(kind, at - lag)

    def drained(kind):
        def body(block, way, onward):
            for m in range(micro):
                each_way(kind, onward, block, m, wait_send)
                if kind >= SIDE:
                    lower_copy(kind, block, m).wait_send()

        for m in range(micro):
            each_way(kind, range(4), q, m, wait_send)
        column_blocks(body)
        row_blocks(body)

    @pl.when(sec == last)
    def _():
        @pl.when(q < n_seq - 1)
        def _():
            c_copy(0).start()

        @pl.when(q > 0)
        def _():
            c_copy(1).start()

        gall[q] = cot_ref[...]
        for m in range(micro):
            each_way(FULL, range(4), q, m, start)
        gradf[:, EDGE + halo : EDGE + halo + rows] = cot_ref[...].astype(F32)

        @pl.when(q == 0)
        def _():
            gradf[:, EDGE : EDGE + halo] = jnp.zeros((micro, halo, chans), F32)

        @pl.when(q == n_seq - 1)
        def _():
            gradf[:, EDGE + halo + rows : EDGE + ext] = jnp.zeros((micro, halo, chans), F32)

        @pl.when(q > 0)
        def _():
            c_copy(0).wait_recv()
            gradf[:, EDGE : EDGE + halo] = coth[0].astype(F32)

        @pl.when(q < n_seq - 1)
        def _():
            c_copy(1).wait_recv()
            gradf[:, EDGE + halo + rows : EDGE + ext] = coth[1].astype(F32)

        w_copy.wait()

        def each(m, carry):
            conv_back(m)
            return carry

        lax.fori_loop(0, micro, each, 0)
        column_blocks(taking(FULL))

    def f_copy(m, kind):
        to = sec + 1 if kind == 0 else mirror_sec
        dst = inflow if kind == 0 else skip
        return remote(fout.at[m], dst.at[m], f_send.at[m, kind], f_recv.at[m, kind], section=to)

    def b_copy(m, kind):
        to = sec - 1 if kind == 0 else mirror_sec
        dst = gin if kind == 0 else gskip
        return remote(gsend.at[m], dst.at[m], b_send.at[m, kind], b_recv.at[m, kind], section=to)

    def by_rows(body):
        def one(i, carry):
            body(pl.multiple_of(i * step, step))
            return carry

        lax.fori_loop(0, ext // step, one, 0, unroll=True)

    def pull_back(m):
        def pull_rows(r):
            at = pl.ds(r, step)
            b, grad = bsum[m, at], gact[m, at]
            scale = lax.rsqrt(jnp.mean(b * b, axis=-1, keepdims=True) + 1e-06)
            unit = b * scale
            x = unit * gain_ref[...]
            t = jnp.tanh(GELU_A * (x + GELU_B * (x * x * x)))
            slope = 0.5 * (1.0 + t) + (0.5 * GELU_A) * x * (1.0 - t * t) * (
                1.0 + (3.0 * GELU_B) * (x * x)
            )
            d_pre = grad * slope
            d_unit = d_pre * gain_ref[...]
            place = lax.broadcasted_iota(jnp.int32, (step, 1), 0) + r
            mine = (place >= halo) & (place < halo + rows)
            terms = jnp.where(mine, d_pre * unit, 0.0)
            gain_acc[...] += jnp.sum(terms.reshape(step // 8, 8, chans), axis=0)
            pulled = scale * (d_unit - unit * jnp.mean(d_unit * unit, axis=-1, keepdims=True))
            whole = gradf[m, pl.ds(pl.multiple_of(EDGE + r, 8), step)] + pulled
            gsend[m, at] = jnp.where(row_mask(r, step), whole, 0.0).astype(BF16)

        by_rows(pull_rows)

        @pl.when(sec > 0)
        def _():
            b_copy(m, 0).start()

            @pl.when(sec > half)
            def _():
                b_copy(m, 1).start()


    def forward(m, carry):
        @pl.when(sec == 0)
        def _():
            tap = lax.broadcasted_iota(jnp.int32, (ext, LANES), 1) // BASES
            hot = jnp.zeros((ext, LANES), F32)
            for k in range(STEM_K):
                off = e_halo - halo + k - (STEM_K - 1) // 2
                hot = jnp.where(tap == k, ebuf[m, off : off + ext], hot)
            stem = jnp.dot(
                hot.astype(BF16), stemf[...].astype(BF16), preferred_element_type=F32
            )
            bsum[m] = stem.astype(BF16).astype(F32)

        @pl.when(sec > 0)
        def _():
            f_copy(m, 0).wait_recv()

            @pl.when(sec < half)
            def _():
                bsum[m] = inflow[m].astype(F32)

            @pl.when(sec == half)
            def _():
                bsum[m] = inflow[m].astype(F32) * 2.0

            @pl.when(sec > half)
            def _():
                f_copy(m, 1).wait_recv()
                bsum[m] = inflow[m].astype(F32) + skip[m].astype(F32)

        @pl.when(sec == last)
        def _():
            pull_back(m)

        def act_rows(r):
            b = bsum[m, pl.ds(r, step)]
            scale = lax.rsqrt(jnp.mean(b * b, axis=-1, keepdims=True) + 1e-06)
            x = b * scale * gain_ref[...]
            t = jnp.tanh(GELU_A * (x + GELU_B * (x * x * x)))
            y = (x * (0.5 * (1.0 + t))).astype(BF16).astype(F32)
            actf[m, pl.ds(pl.multiple_of(EDGE + r, 8), step)] = jnp.where(row_mask(r, step), y, 0.0)

        by_rows(act_rows)

        @pl.when(sec < last)
        def _():
            shifted(actf, m, False)

            @pl.when(m == 0)
            def _():
                w_copy.wait()

            def tile(n, c):
                at = pl.ds(pl.multiple_of(n * 256, 256), 256)
                total = bsum[m, :, at] + jnp.dot(
                    x5[...], w_ref[:, at], preferred_element_type=F32
                )
                fout[m, :, at] = total.astype(BF16)
                return c

            lax.fori_loop(0, chans // 256, tile, 0)
            f_copy(m, 0).start()

            @pl.when(sec < half - 1)
            def _():
                f_copy(m, 1).start()

        return carry

    lax.fori_loop(0, micro, forward, 0)

    def picker(j):
        c = lax.broadcasted_iota(jnp.int32, (chans, LANES), 0)
        lane = lax.broadcasted_iota(jnp.int32, (chans, LANES), 1)
        return jnp.where((c == j * part + lane) & (lane < part), 1.0, 0.0).astype(BF16)

    def a_copy(j):
        return remote(aslab.at[j], acol.at[q], a_send.at[j], a_recv.at[q], seq=j)

    def a_from(j):
        return remote(aslab.at[j], acol.at[j], a_send.at[j], a_recv.at[j], seq=j)

    def spread_rows():
        own = slice(EDGE + halo, EDGE + halo + rows)

        def slab(j, carry):
            pick = picker(j)
            for m in range(micro):
                aslab[j, m] = jnp.dot(
                    actf[m, own].astype(BF16), pick, preferred_element_type=F32
                ).astype(BF16)

            @pl.when(j != q)
            def _():
                a_copy(j).start()

            @pl.when(j == q)
            def _():
                acol[j] = aslab[j]

            return carry

        lax.fori_loop(0, n_seq, slab, 0)

        def take(j, carry):
            @pl.when(j != q)
            def _():
                a_from(j).wait_recv()

            at = pl.ds(pl.multiple_of(EDGE + j * rows, 8), rows)
            for m in range(micro):
                acolf[m, at] = acol[j, m].astype(F32)
            return carry

        lax.fori_loop(0, n_seq, take, 0)

        eye = jnp.where(
            lax.broadcasted_iota(jnp.int32, (LANES, LANES), 0)
            == lax.broadcasted_iota(jnp.int32, (LANES, LANES), 1), 1.0, 0.0,
        ).astype(BF16)

        def turn(j, carry):
            for m in range(micro):
                window = acolf[m, pl.ds(pl.multiple_of(j * rows, rows), rows + 2 * EDGE)]
                for k in range(KERNEL):
                    off = EDGE + k - reach
                    a5t[j, k * LANES : (k + 1) * LANES, m * rows : (m + 1) * rows] = (
                        lax.dot_general(
                            eye, window[off : off + rows].astype(BF16),
                            (((1,), (1,)), ((), ())), preferred_element_type=F32,
                        ).astype(BF16)
                    )
            return carry

        lax.fori_loop(0, n_seq, turn, 0)

    @pl.when(sec < half)
    def _():
        spread_rows()

    def backward(m, carry):
        b_copy(m, 0).wait_recv()

        @pl.when(sec < half - 1)
        def _():
            b_copy(m, 1).wait_recv()
            gradf[m, EDGE : EDGE + ext] = (
                (gin[m].astype(F32) + gskip[m].astype(F32)).astype(BF16).astype(F32)
            )

        @pl.when(sec == half - 1)
        def _():
            gradf[m, EDGE : EDGE + ext] = gin[m].astype(F32) * 2.0

        @pl.when(sec >= half)
        def _():
            gradf[m, EDGE : EDGE + ext] = gin[m].astype(F32)

        gall[q, m] = gradf[m, EDGE + halo : EDGE + halo + rows].astype(BF16)

        @pl.when(sec < half)
        def _():
            each_way(MAIN, range(4), q, m, start)

            @pl.when(sec > 0)
            def _():
                raise_copy(SIDE, m).start()

            @pl.when(sec == 0)
            def _():
                raise_copy(FIRST, m).start()

        @pl.when(sec >= half)
        def _():
            each_way(FULL, range(4), q, m, start)

        conv_back(m)
        pull_back(m)
        return carry

    @pl.when(sec < last)
    def _():
        lax.fori_loop(0, micro, backward, 0)

    @pl.when(sec >= half)
    def _():
        @pl.when(sec < last)
        def _():
            column_blocks(taking(FULL))

        spread_rows()

        if last > half + 1:
            @pl.when((sec > half) & (sec < last))
            def _():
                relay((SIDE,))

        @pl.when(sec == last)
        def _():
            relay((SIDE, FIRST))

    def n_copy(j):
        return remote(gslab.at[j], grecv.at[q], n_send.at[j], n_recv.at[q], seq=j)

    def n_from(j):
        return remote(gslab.at[j], grecv.at[j], n_send.at[j], n_recv.at[j], seq=j)

    gain_part = jnp.broadcast_to(jnp.sum(gain_acc[...], axis=0, keepdims=True), (16, chans))
    gain_part = gain_part.astype(BF16)

    def gain_slab(j, carry):
        gslab[j] = jnp.dot(gain_part, picker(j), preferred_element_type=F32)[0:8]

        @pl.when(j != q)
        def _():
            n_copy(j).start()

        @pl.when(j == q)
        def _():
            grecv[j] = gslab[j]

        return carry

    lax.fori_loop(0, n_seq, gain_slab, 0)

    multiply(q)

    @pl.when(sec < half)
    def _():
        column_blocks(taking(MAIN))
        column_blocks(joined)
        row_blocks(taking(MAIN, joined))

    @pl.when(sec >= half)
    def _():
        column_blocks(lambda block, way, onward: multiply(block))
        row_blocks(taking(FULL, multiply))

    for k in range(KERNEL):
        out_ref[k] = acc[k * LANES : k * LANES + part].astype(BF16)

    def gain_take(j, total):
        @pl.when(j != q)
        def _():
            n_from(j).wait_recv()

        return total + grecv[j]

    gain_total = lax.fori_loop(0, n_seq, gain_take, jnp.zeros((8, LANES), F32))
    gout_ref[...] = gain_total[0:1, 0:part]

    @pl.when(sec == 0)
    def _():
        @pl.when(q < n_seq - 1)
        def _():
            e_copy(0).wait_send()

        @pl.when(q > 0)
        def _():
            e_copy(1).wait_send()

    @pl.when(sec == last)
    def _():
        @pl.when(q < n_seq - 1)
        def _():
            c_copy(0).wait_send()

        @pl.when(q > 0)
        def _():
            c_copy(1).wait_send()

    for m in range(micro):
        @pl.when(sec < last)
        def _():
            f_copy(m, 0).wait_send()

        @pl.when(sec < half - 1)
        def _():
            f_copy(m, 1).wait_send()

        @pl.when(sec > 0)
        def _():
            b_copy(m, 0).wait_send()

        @pl.when(sec > half)
        def _():
            b_copy(m, 1).wait_send()

        @pl.when(sec < half)
        def _():
            raise_copy(SIDE, m).wait_send()

    @pl.when(sec < half)
    def _():
        drained(MAIN)

    @pl.when(sec >= half)
    def _():
        drained(FULL)

        @pl.when(sec > half)
        def _():
            drained(SIDE)

        @pl.when(sec == last)
        def _():
            drained(FIRST)

    def sent(j, carry):
        @pl.when(j != q)
        def _():
            a_copy(j).wait_send()
            n_copy(j).wait_send()

        return carry

    lax.fori_loop(0, n_seq, sent, 0)


def finish(conv_ref, gain_ref, out_ref, gout_ref):
    out_ref[0] = conv_ref[...]
    gout_ref[...] = gain_ref[...]


def shards(sections, n_seq, base_ids, stem_weight, conv_weight, block_gain, cotangent):
    micro, rows, chans = cotangent.shape
    n_lo = max(1, n_seq // 4)
    halo = -(-4 * (sections - 1) // 16) * 16
    ext = rows + 2 * halo
    e_halo = halo + 16
    part = chans // n_seq
    vmem, dma = pltpu.VMEM, pltpu.SemaphoreType.DMA
    flow = vmem((micro, ext, chans), BF16)
    scratch = [
        vmem((KERNEL * chans, chans), BF16),
        vmem((LANES, chans), F32),
        vmem((micro, rows + 2 * e_halo, LANES), F32),
        vmem((micro, ext, chans), F32),
        vmem((micro, ext + 2 * EDGE, chans), F32),
        vmem((ext, KERNEL * chans), BF16),
        vmem((micro, ext + 2 * EDGE, chans), F32),
        vmem((micro, ext, chans), F32),
        flow, flow, flow, flow, flow, flow,
        vmem((2, micro, halo, chans), BF16),
        vmem((n_seq, micro, rows, LANES), BF16),
        vmem((n_seq, micro, rows, LANES), BF16),
        vmem((micro, n_seq * rows + 2 * EDGE, LANES), F32),
        vmem((n_seq, KERNEL * LANES, micro * rows), BF16),
        vmem((n_seq, micro, rows, chans), BF16),
        vmem((KERNEL * LANES, chans), F32),
        vmem((8, chans), F32),
        vmem((n_seq, 8, LANES), F32),
        vmem((n_seq, 8, LANES), F32),
        dma((2,)), dma((2,)), dma((2,)), dma((2,)),
        dma((micro, 2)), dma((micro, 2)), dma((micro, 2)), dma((micro, 2)),
        dma((n_seq,)), dma((n_seq,)), dma((n_seq,)), dma((n_seq,)),
        dma((n_seq, micro, 4)), dma((n_seq, micro)), dma,
        vmem((2, n_seq, micro, rows, chans - chans * 2 // 3 // LANES * LANES), BF16),
        dma((2, n_seq, micro, 4)), dma((2, n_seq, micro)), dma((micro,)), dma((2, micro)),
        dma((2, n_seq, micro)), dma((n_seq, micro)),
    ]
    conv_grad, gain_grad = pl.pallas_call(
        functools.partial(level_kernel, sections, n_seq, n_lo, micro, rows, chans, halo),
        out_shape=(
            jax.ShapeDtypeStruct((KERNEL, part, chans), BF16),
            jax.ShapeDtypeStruct((1, part), F32),
        ),
        in_specs=[pl.BlockSpec(memory_space=pl.ANY if i == 2 else vmem) for i in range(5)],
        out_specs=(pl.BlockSpec(memory_space=pltpu.VMEM),) * 2,
        scratch_shapes=scratch,
        compiler_params=pltpu.CompilerParams(
            collective_id=0, has_side_effects=True, vmem_limit_bytes=58 * 2**20
        ),
    )(base_ids, stem_weight, conv_weight[0].reshape(KERNEL * chans, chans), block_gain, cotangent)
    whole = pl.BlockSpec(memory_space=vmem)
    conv_grad, gain_grad = pl.pallas_call(
        finish,
        out_shape=(
            jax.ShapeDtypeStruct((1, KERNEL, part, chans), BF16),
            jax.ShapeDtypeStruct((1, part), F32),
        ),
        in_specs=[whole, whole],
        out_specs=(whole, whole),
    )(conv_grad, gain_grad)
    return conv_grad, gain_grad


def solution(mesh):
    placed = (
        P(None, "seq"),
        P(),
        P("section", None, None, None),
        P("section", None),
        P(None, "seq", None),
    )
    return jax.shard_map(
        functools.partial(shards, mesh.shape["section"], mesh.shape["seq"]),
        mesh=mesh,
        in_specs=placed,
        out_specs=(P("section", None, "seq", None), P("section", "seq")),
        check_vma=False,
    )
```

```python
import functools

import jax
import jax.numpy as jnp
from jax import lax
from jax.experimental import pallas as pl
from jax.experimental.pallas import tpu as pltpu
from jax.sharding import PartitionSpec as P

KERNEL = 5
STEM_K = 15
BASES = 4
LANES = 128
EDGE = 8
F32, BF16 = jnp.float32, jnp.bfloat16
FULL, MAIN, SIDE, FIRST = 0, 1, 2, 3
GELU_A, GELU_B = 0.7978845608028654, 0.044715


def remote(src, dst, send_sem, recv_sem, **where):
    return pltpu.make_async_remote_copy(
        src_ref=src,
        dst_ref=dst,
        send_sem=send_sem,
        recv_sem=recv_sem,
        device_id=where,
        device_id_type=pl.DeviceIdType.MESH,
    )


def level_kernel(
    sections, n_seq, n_lo, micro, rows, chans, halo,
    ids_ref, stem_ref, w_hbm, gain_ref, cot_ref,
    out_ref, gout_ref,
    w_ref, stemf, ebuf, bsum, actf, x5, gradf, gact, inflow, skip, fout, gin, gskip, gsend, coth,
    aslab, acol, acolf, a5t, gall, acc, gain_acc, gslab, grecv,
    e_send, e_recv, c_send, c_recv, f_send, f_recv, b_send, b_recv,
    a_send, a_recv, n_send, n_recv, ag_send, ag_recv, w_sem,
    rbuf, r_send, r_recv, u_send, u_recv, d_send, d_recv,
):
    sec, q = lax.axis_index("section"), lax.axis_index("seq")
    n_hi = n_seq // n_lo
    shared = (sec > 0) & (sec < sections // 2)
    hi, lo = q // n_lo, q % n_lo
    half = sections // 2
    ext = rows + 2 * halo
    e_halo = halo + 16
    part = chans // n_seq
    reach = (KERNEL - 1) // 2
    cut = chans * 2 // 3 // LANES * LANES
    last = sections - 1
    mirror_sec = last - sec
    step = 32
    tokens = rows * n_seq

    w_copy = pltpu.make_async_copy(w_hbm, w_ref, w_sem)
    w_copy.start()
    barrier = pltpu.get_barrier_semaphore()
    for d in range(1, n_seq):
        pl.semaphore_signal(
            barrier, inc=1, device_id={"seq": (q + d) % n_seq}, device_id_type=pl.DeviceIdType.MESH
        )
    for d in range(1, sections):
        pl.semaphore_signal(
            barrier, inc=1, device_id={"section": (sec + d) % sections},
            device_id_type=pl.DeviceIdType.MESH,
        )
    pl.semaphore_wait(barrier, n_seq + sections - 2)

    def e_copy(side):
        if side == 0:
            src, dst, to = ebuf.at[:, rows : e_halo + rows], ebuf.at[:, 0:e_halo], q + 1
        else:
            src, dst, to = ebuf.at[:, e_halo : 2 * e_halo], ebuf.at[:, e_halo + rows :], q - 1
        return remote(src, dst, e_send.at[side], e_recv.at[side], seq=to)

    def c_copy(side):
        if side == 0:
            src, dst, to = cot_ref.at[:, rows - halo : rows], coth.at[0], q + 1
        else:
            src, dst, to = cot_ref.at[:, 0:halo], coth.at[1], q - 1
        return remote(src, dst, c_send.at[side], c_recv.at[side], seq=to)

    def gather_copy(kind, block, m, way):
        to = [q + n_lo, q - n_lo, q + 1, q - 1][way]
        if kind >= SIDE:
            slot = kind - SIDE
            here, sends, lands = rbuf.at[slot, block, m], r_send.at[slot], r_recv.at[slot]
        else:
            here = gall.at[block, m] if kind == FULL else gall.at[block, m, :, 0:cut]
            sends, lands = ag_send, ag_recv
        return remote(here, here, sends.at[block, m, way], lands.at[block, m], seq=to)

    def raise_copy(kind, m):
        slot = kind - SIDE
        return remote(
            gall.at[q, m, :, cut:], rbuf.at[slot, q, m], u_send.at[m], u_recv.at[slot, m],
            section=last if kind == FIRST else sec + half,
        )

    def lower_copy(kind, block, m):
        slot = kind - SIDE
        return remote(
            rbuf.at[slot, block, m], gall.at[block, m, :, cut:], d_send.at[slot, block, m],
            d_recv.at[block, m], section=0 if kind == FIRST else sec - half,
        )

    up, down, right, left = hi < n_hi - 1, hi > 0, lo < n_lo - 1, lo > 0

    def each_way(kind, ways, block, m, act):
        for way in ways:
            @pl.when([up, down, right, left][way])
            def _():
                act(gather_copy(kind, block, m, way))

    def start(copy):
        copy.start()

    def wait_send(copy):
        copy.wait_send()

    for ref in (actf, gradf):
        ref[:, 0:EDGE] = jnp.zeros((micro, EDGE, chans), F32)
        ref[:, EDGE + ext :] = jnp.zeros((micro, EDGE, chans), F32)
    acolf[:, 0:EDGE] = jnp.zeros((micro, EDGE, LANES), F32)
    acolf[:, EDGE + tokens :] = jnp.zeros((micro, EDGE, LANES), F32)
    gain_acc[...] = jnp.zeros_like(gain_acc)
    acc[...] = jnp.zeros_like(acc)

    @pl.when(sec == 0)
    def _():
        lane = lax.broadcasted_iota(jnp.int32, (rows, LANES), 1)
        wanted = jnp.where(lane < STEM_K * BASES, lane % BASES, -1).astype(F32)
        for m in range(micro):
            ids = jnp.broadcast_to(ids_ref[m : m + 1, :].astype(F32), (LANES, rows)).T
            ebuf[m, e_halo : e_halo + rows] = jnp.where(ids == wanted, 1.0, 0.0)

        @pl.when(q < n_seq - 1)
        def _():
            e_copy(0).start()

        @pl.when(q > 0)
        def _():
            e_copy(1).start()

        stemf[...] = jnp.zeros_like(stemf)
        for k in range(STEM_K):
            stemf[k * BASES : (k + 1) * BASES] = stem_ref[k].astype(F32)

        @pl.when(q == 0)
        def _():
            ebuf[:, 0:e_halo] = jnp.zeros((micro, e_halo, LANES), F32)

        @pl.when(q == n_seq - 1)
        def _():
            ebuf[:, e_halo + rows :] = jnp.zeros((micro, e_halo, LANES), F32)

        @pl.when(q > 0)
        def _():
            e_copy(0).wait_recv()

        @pl.when(q < n_seq - 1)
        def _():
            e_copy(1).wait_recv()

    def row_mask(first, count):
        place = lax.broadcasted_iota(jnp.int32, (count, 1), 0) + (first + q * rows - halo)
        return (place >= 0) & (place < tokens)

    def shifted(ref, m, flip):
        for k in range(KERNEL):
            off = EDGE + (reach - k if flip else k - reach)
            x5[:, k * chans : (k + 1) * chans] = ref[m, off : off + ext].astype(BF16)

    def conv_back(m):
        shifted(gradf, m, True)

        def tile(n, carry):
            at = pl.ds(pl.multiple_of(n * 256, 256), 256)
            total = jnp.zeros((ext, 256), F32)
            for k in range(KERNEL):
                total = total + lax.dot_general(
                    x5[:, k * chans : (k + 1) * chans],
                    w_ref[pl.ds(pl.multiple_of(k * chans + n * 256, 256), 256), :],
                    (((1,), (1,)), ((), ())),
                    preferred_element_type=F32,
                )
            gact[m, :, at] = total
            return carry

        lax.fori_loop(0, chans // 256, tile, 0)

    def multiply(block):
        def tile(n, c):
            at = pl.ds(pl.multiple_of(n * 256, 256), 256)
            acc[:, at] += jnp.dot(
                a5t[block], gall[block, :, :, at].reshape(micro * rows, 256),
                preferred_element_type=F32,
            )
            return c

        lax.fori_loop(0, chans // 256, tile, 0)

    def column_blocks(body, distances=range(1, n_hi)):
        for d in distances:
            @pl.when(hi - d >= 0)
            def _():
                body(q - d * n_lo, 0, (0, 2, 3))

            @pl.when(hi + d < n_hi)
            def _():
                body(q + d * n_lo, 1, (1, 2, 3))

    def row_blocks(body):
        for e in range(1, n_lo):
            for d in range(n_hi):
                for side in (-1, 1) if d else (1,):
                    h = hi + side * d

                    @pl.when((h >= 0) & (h < n_hi) & (lo - e >= 0))
                    def _():
                        body(h * n_lo + lo - e, 2, (2,))

                    @pl.when((h >= 0) & (h < n_hi) & (lo + e < n_lo))
                    def _():
                        body(h * n_lo + lo + e, 3, (3,))

    def taking(kind, then=None):
        def body(block, way, onward):
            for m in range(micro):
                gather_copy(kind, block, m, way).wait_recv()
                each_way(kind, onward, block, m, start)
                if kind >= SIDE:
                    lower_copy(kind, block, m).start()
            if then is not None:
                then(block)

        return body

    def joined(block, way=0, onward=()):
        for m in range(micro):
            remote(
                rbuf.at[0, block, m], gall.at[block, m, :, cut:], d_send.at[0, block, m],
                d_recv.at[block, m], section=last,
            ).wait_recv()
        multiply(block)

    def relay(kinds):
        def stage(kind, at):
            if at == 0:
                for m in range(micro):
                    raise_copy(kind, m).wait_recv()
                    each_way(kind, range(4), q, m, start)
            elif at < n_hi:
                column_blocks(taking(kind), (at,))
            elif at == n_hi:
                row_blocks(taking(kind))

        for at in range(n_hi + len(kinds)):
            for lag, kind in enumerate(kinds):
                if at >= lag:
                    stage(kind, at - lag)

    def drained(kind):
        def body(block, way, onward):
            for m in range(micro):
                each_way(kind, onward, block, m, wait_send)
                if kind >= SIDE:
                    lower_copy(kind, block, m).wait_send()

        for m in range(micro):
            each_way(kind, range(4), q, m, wait_send)
        column_blocks(body)
        row_blocks(body)

    @pl.when(sec == last)
    def _():
        @pl.when(q < n_seq - 1)
        def _():
            c_copy(0).start()

        @pl.when(q > 0)
        def _():
            c_copy(1).start()

        gall[q] = cot_ref[...]
        for m in range(micro):
            each_way(FULL, range(4), q, m, start)
        gradf[:, EDGE + halo : EDGE + halo + rows] = cot_ref[...].astype(F32)

        @pl.when(q == 0)
        def _():
            gradf[:, EDGE : EDGE + halo] = jnp.zeros((micro, halo, chans), F32)

        @pl.when(q == n_seq - 1)
        def _():
            gradf[:, EDGE + halo + rows : EDGE + ext] = jnp.zeros((micro, halo, chans), F32)

        @pl.when(q > 0)
        def _():
            c_copy(0).wait_recv()
            gradf[:, EDGE : EDGE + halo] = coth[0].astype(F32)

        @pl.when(q < n_seq - 1)
        def _():
            c_copy(1).wait_recv()
            gradf[:, EDGE + halo + rows : EDGE + ext] = coth[1].astype(F32)

        w_copy.wait()

        def each(m, carry):
            conv_back(m)
            return carry

        lax.fori_loop(0, micro, each, 0)
        column_blocks(taking(FULL))

    def f_copy(m, kind):
        to = sec + 1 if kind == 0 else mirror_sec
        dst = inflow if kind == 0 else skip
        return remote(fout.at[m], dst.at[m], f_send.at[m, kind], f_recv.at[m, kind], section=to)

    def b_copy(m, kind):
        to = sec - 1 if kind == 0 else mirror_sec
        dst = gin if kind == 0 else gskip
        return remote(gsend.at[m], dst.at[m], b_send.at[m, kind], b_recv.at[m, kind], section=to)

    def by_rows(body):
        def one(i, carry):
            body(pl.multiple_of(i * step, step))
            return carry

        lax.fori_loop(0, ext // step, one, 0, unroll=True)

    def pull_back(m):
        def pull_rows(r):
            at = pl.ds(r, step)
            b, grad = bsum[m, at], gact[m, at]
            scale = lax.rsqrt(jnp.mean(b * b, axis=-1, keepdims=True) + 1e-06)
            unit = b * scale
            x = unit * gain_ref[...]
            t = jnp.tanh(GELU_A * (x + GELU_B * (x * x * x)))
            slope = 0.5 * (1.0 + t) + (0.5 * GELU_A) * x * (1.0 - t * t) * (
                1.0 + (3.0 * GELU_B) * (x * x)
            )
            d_pre = grad * slope
            d_unit = d_pre * gain_ref[...]
            place = lax.broadcasted_iota(jnp.int32, (step, 1), 0) + r
            mine = (place >= halo) & (place < halo + rows)
            terms = jnp.where(mine, d_pre * unit, 0.0)
            gain_acc[...] += jnp.sum(terms.reshape(step // 8, 8, chans), axis=0)
            pulled = scale * (d_unit - unit * jnp.mean(d_unit * unit, axis=-1, keepdims=True))
            whole = gradf[m, pl.ds(pl.multiple_of(EDGE + r, 8), step)] + pulled
            gsend[m, at] = jnp.where(row_mask(r, step), whole, 0.0).astype(BF16)

        by_rows(pull_rows)

        @pl.when(sec > 0)
        def _():
            b_copy(m, 0).start()

            @pl.when(sec > half)
            def _():
                b_copy(m, 1).start()


    def forward(m, carry):
        @pl.when(sec == 0)
        def _():
            tap = lax.broadcasted_iota(jnp.int32, (ext, LANES), 1) // BASES
            hot = jnp.zeros((ext, LANES), F32)
            for k in range(STEM_K):
                off = e_halo - halo + k - (STEM_K - 1) // 2
                hot = jnp.where(tap == k, ebuf[m, off : off + ext], hot)
            stem = jnp.dot(
                hot.astype(BF16), stemf[...].astype(BF16), preferred_element_type=F32
            )
            bsum[m] = stem.astype(BF16).astype(F32)

        @pl.when(sec > 0)
        def _():
            f_copy(m, 0).wait_recv()

            @pl.when(sec < half)
            def _():
                bsum[m] = inflow[m].astype(F32)

            @pl.when(sec == half)
            def _():
                bsum[m] = inflow[m].astype(F32) * 2.0

            @pl.when(sec > half)
            def _():
                f_copy(m, 1).wait_recv()
                bsum[m] = inflow[m].astype(F32) + skip[m].astype(F32)

        @pl.when(sec == last)
        def _():
            pull_back(m)

        def act_rows(r):
            b = bsum[m, pl.ds(r, step)]
            scale = lax.rsqrt(jnp.mean(b * b, axis=-1, keepdims=True) + 1e-06)
            x = b * scale * gain_ref[...]
            t = jnp.tanh(GELU_A * (x + GELU_B * (x * x * x)))
            y = (x * (0.5 * (1.0 + t))).astype(BF16).astype(F32)
            actf[m, pl.ds(pl.multiple_of(EDGE + r, 8), step)] = jnp.where(row_mask(r, step), y, 0.0)

        by_rows(act_rows)

        @pl.when(sec < last)
        def _():
            shifted(actf, m, False)

            @pl.when(m == 0)
            def _():
                w_copy.wait()

            def tile(n, c):
                at = pl.ds(pl.multiple_of(n * 256, 256), 256)
                total = bsum[m, :, at] + jnp.dot(
                    x5[...], w_ref[:, at], preferred_element_type=F32
                )
                fout[m, :, at] = total.astype(BF16)
                return c

            lax.fori_loop(0, chans // 256, tile, 0)
            f_copy(m, 0).start()

            @pl.when(sec < half - 1)
            def _():
                f_copy(m, 1).start()

        return carry

    lax.fori_loop(0, micro, forward, 0)

    def picker(j):
        c = lax.broadcasted_iota(jnp.int32, (chans, LANES), 0)
        lane = lax.broadcasted_iota(jnp.int32, (chans, LANES), 1)
        return jnp.where((c == j * part + lane) & (lane < part), 1.0, 0.0).astype(BF16)

    def a_copy(j):
        return remote(aslab.at[j], acol.at[q], a_send.at[j], a_recv.at[q], seq=j)

    def a_from(j):
        return remote(aslab.at[j], acol.at[j], a_send.at[j], a_recv.at[j], seq=j)

    def spread_rows():
        own = slice(EDGE + halo, EDGE + halo + rows)

        def slab(j, carry):
            pick = picker(j)
            for m in range(micro):
                aslab[j, m] = jnp.dot(
                    actf[m, own].astype(BF16), pick, preferred_element_type=F32
                ).astype(BF16)

            @pl.when(j != q)
            def _():
                a_copy(j).start()

            @pl.when(j == q)
            def _():
                acol[j] = aslab[j]

            return carry

        lax.fori_loop(0, n_seq, slab, 0)

        def take(j, carry):
            @pl.when(j != q)
            def _():
                a_from(j).wait_recv()

            at = pl.ds(pl.multiple_of(EDGE + j * rows, 8), rows)
            for m in range(micro):
                acolf[m, at] = acol[j, m].astype(F32)
            return carry

        lax.fori_loop(0, n_seq, take, 0)

        eye = jnp.where(
            lax.broadcasted_iota(jnp.int32, (LANES, LANES), 0)
            == lax.broadcasted_iota(jnp.int32, (LANES, LANES), 1), 1.0, 0.0,
        ).astype(BF16)

        def turn(j, carry):
            for m in range(micro):
                window = acolf[m, pl.ds(pl.multiple_of(j * rows, rows), rows + 2 * EDGE)]
                for k in range(KERNEL):
                    off = EDGE + k - reach
                    a5t[j, k * LANES : (k + 1) * LANES, m * rows : (m + 1) * rows] = (
                        lax.dot_general(
                            eye, window[off : off + rows].astype(BF16),
                            (((1,), (1,)), ((), ())), preferred_element_type=F32,
                        ).astype(BF16)
                    )
            return carry

        lax.fori_loop(0, n_seq, turn, 0)

    @pl.when(sec < half)
    def _():
        spread_rows()

    def backward(m, carry):
        b_copy(m, 0).wait_recv()

        @pl.when(sec < half - 1)
        def _():
            b_copy(m, 1).wait_recv()
            gradf[m, EDGE : EDGE + ext] = (
                (gin[m].astype(F32) + gskip[m].astype(F32)).astype(BF16).astype(F32)
            )

        @pl.when(sec == half - 1)
        def _():
            gradf[m, EDGE : EDGE + ext] = gin[m].astype(F32) * 2.0

        @pl.when(sec >= half)
        def _():
            gradf[m, EDGE : EDGE + ext] = gin[m].astype(F32)

        gall[q, m] = gradf[m, EDGE + halo : EDGE + halo + rows].astype(BF16)

        @pl.when(shared)
        def _():
            each_way(MAIN, range(4), q, m, start)
            raise_copy(SIDE, m).start()

        @pl.when(jnp.logical_not(shared))
        def _():
            each_way(FULL, range(4), q, m, start)

        conv_back(m)
        pull_back(m)
        return carry

    @pl.when(sec < last)
    def _():
        lax.fori_loop(0, micro, backward, 0)

    @pl.when(sec >= half)
    def _():
        @pl.when(sec < last)
        def _():
            column_blocks(taking(FULL))

        spread_rows()

        @pl.when(sec > half)
        def _():
            relay((SIDE,))

    def n_copy(j):
        return remote(gslab.at[j], grecv.at[q], n_send.at[j], n_recv.at[q], seq=j)

    def n_from(j):
        return remote(gslab.at[j], grecv.at[j], n_send.at[j], n_recv.at[j], seq=j)

    gain_part = jnp.broadcast_to(jnp.sum(gain_acc[...], axis=0, keepdims=True), (16, chans))
    gain_part = gain_part.astype(BF16)

    def gain_slab(j, carry):
        gslab[j] = jnp.dot(gain_part, picker(j), preferred_element_type=F32)[0:8]

        @pl.when(j != q)
        def _():
            n_copy(j).start()

        @pl.when(j == q)
        def _():
            grecv[j] = gslab[j]

        return carry

    lax.fori_loop(0, n_seq, gain_slab, 0)

    multiply(q)

    @pl.when(sec == 0)
    def _():
        column_blocks(taking(FULL))
        column_blocks(lambda block, way, onward: multiply(block))
        row_blocks(taking(FULL, multiply))

    @pl.when(shared)
    def _():
        column_blocks(taking(MAIN))
        column_blocks(joined)
        row_blocks(taking(MAIN, joined))

    @pl.when(sec >= half)
    def _():
        column_blocks(lambda block, way, onward: multiply(block))
        row_blocks(taking(FULL, multiply))

    for k in range(KERNEL):
        out_ref[k] = acc[k * LANES : k * LANES + part].astype(BF16)

    def gain_take(j, total):
        @pl.when(j != q)
        def _():
            n_from(j).wait_recv()

        return total + grecv[j]

    gain_total = lax.fori_loop(0, n_seq, gain_take, jnp.zeros((8, LANES), F32))
    gout_ref[...] = gain_total[0:1, 0:part]

    @pl.when(sec == 0)
    def _():
        @pl.when(q < n_seq - 1)
        def _():
            e_copy(0).wait_send()

        @pl.when(q > 0)
        def _():
            e_copy(1).wait_send()

    @pl.when(sec == last)
    def _():
        @pl.when(q < n_seq - 1)
        def _():
            c_copy(0).wait_send()

        @pl.when(q > 0)
        def _():
            c_copy(1).wait_send()

    for m in range(micro):
        @pl.when(sec < last)
        def _():
            f_copy(m, 0).wait_send()

        @pl.when(sec < half - 1)
        def _():
            f_copy(m, 1).wait_send()

        @pl.when(sec > 0)
        def _():
            b_copy(m, 0).wait_send()

        @pl.when(sec > half)
        def _():
            b_copy(m, 1).wait_send()

        @pl.when(shared)
        def _():
            raise_copy(SIDE, m).wait_send()

    @pl.when(shared)
    def _():
        drained(MAIN)

    @pl.when(jnp.logical_not(shared))
    def _():
        drained(FULL)

    @pl.when(sec > half)
    def _():
        drained(SIDE)

    def sent(j, carry):
        @pl.when(j != q)
        def _():
            a_copy(j).wait_send()
            n_copy(j).wait_send()

        return carry

    lax.fori_loop(0, n_seq, sent, 0)


def finish(conv_ref, gain_ref, out_ref, gout_ref):
    out_ref[0] = conv_ref[...]
    gout_ref[...] = gain_ref[...]


def shards(sections, n_seq, base_ids, stem_weight, conv_weight, block_gain, cotangent):
    micro, rows, chans = cotangent.shape
    n_lo = max(1, n_seq // 4)
    halo = -(-4 * (sections - 1) // 16) * 16
    ext = rows + 2 * halo
    e_halo = halo + 16
    part = chans // n_seq
    vmem, dma = pltpu.VMEM, pltpu.SemaphoreType.DMA
    flow = vmem((micro, ext, chans), BF16)
    scratch = [
        vmem((KERNEL * chans, chans), BF16),
        vmem((LANES, chans), F32),
        vmem((micro, rows + 2 * e_halo, LANES), F32),
        vmem((micro, ext, chans), F32),
        vmem((micro, ext + 2 * EDGE, chans), F32),
        vmem((ext, KERNEL * chans), BF16),
        vmem((micro, ext + 2 * EDGE, chans), F32),
        vmem((micro, ext, chans), F32),
        flow, flow, flow, flow, flow, flow,
        vmem((2, micro, halo, chans), BF16),
        vmem((n_seq, micro, rows, LANES), BF16),
        vmem((n_seq, micro, rows, LANES), BF16),
        vmem((micro, n_seq * rows + 2 * EDGE, LANES), F32),
        vmem((n_seq, KERNEL * LANES, micro * rows), BF16),
        vmem((n_seq, micro, rows, chans), BF16),
        vmem((KERNEL * LANES, chans), F32),
        vmem((8, chans), F32),
        vmem((n_seq, 8, LANES), F32),
        vmem((n_seq, 8, LANES), F32),
        dma((2,)), dma((2,)), dma((2,)), dma((2,)),
        dma((micro, 2)), dma((micro, 2)), dma((micro, 2)), dma((micro, 2)),
        dma((n_seq,)), dma((n_seq,)), dma((n_seq,)), dma((n_seq,)),
        dma((n_seq, micro, 4)), dma((n_seq, micro)), dma,
        vmem((2, n_seq, micro, rows, chans - chans * 2 // 3 // LANES * LANES), BF16),
        dma((2, n_seq, micro, 4)), dma((2, n_seq, micro)), dma((micro,)), dma((2, micro)),
        dma((2, n_seq, micro)), dma((n_seq, micro)),
    ]
    conv_grad, gain_grad = pl.pallas_call(
        functools.partial(level_kernel, sections, n_seq, n_lo, micro, rows, chans, halo),
        out_shape=(
            jax.ShapeDtypeStruct((KERNEL, part, chans), BF16),
            jax.ShapeDtypeStruct((1, part), F32),
        ),
        in_specs=[pl.BlockSpec(memory_space=pl.ANY if i == 2 else vmem) for i in range(5)],
        out_specs=(pl.BlockSpec(memory_space=pltpu.VMEM),) * 2,
        scratch_shapes=scratch,
        compiler_params=pltpu.CompilerParams(
            collective_id=0, has_side_effects=True, vmem_limit_bytes=58 * 2**20
        ),
    )(base_ids, stem_weight, conv_weight[0].reshape(KERNEL * chans, chans), block_gain, cotangent)
    whole = pl.BlockSpec(memory_space=vmem)
    conv_grad, gain_grad = pl.pallas_call(
        finish,
        out_shape=(
            jax.ShapeDtypeStruct((1, KERNEL, part, chans), BF16),
            jax.ShapeDtypeStruct((1, part), F32),
        ),
        in_specs=[whole, whole],
        out_specs=(whole, whole),
    )(conv_grad, gain_grad)
    return conv_grad, gain_grad


def solution(mesh):
    placed = (
        P(None, "seq"),
        P(),
        P("section", None, None, None),
        P("section", None),
        P(None, "seq", None),
    )
    return jax.shard_map(
        functools.partial(shards, mesh.shape["section"], mesh.shape["seq"]),
        mesh=mesh,
        in_specs=placed,
        out_specs=(P("section", None, "seq", None), P("section", "seq")),
        check_vma=False,
    )
```
